512 devices in a mesh: dp: 32 (over x, y), expert: 16 (over z, core).
Axes of the slice: x: 4, y: 8, z: 8, core: 2. Of those that a mesh axis runs over, the one named last changes fastest.
Arguments:
- tokens: bfloat16 [32768, 2048], P(('dp', 'expert')), may hold values from -6 to 6
- routes: int32 [32768, 8], P(('dp', 'expert')), may hold values from 0 to 127, all different within a row; in each aligned block of 64 rows (0 to 63, 64 to 127, ...) at most 6 rows name the same one
- route_weights: float32 [32768, 8], P(('dp', 'expert')), may hold values from 0.05 to 0.5
- gate_weight: bfloat16 [32, 16, 192, 2048], P('dp', 'expert'), may hold values from -0.125 to 0.125
- up_weight: bfloat16 [32, 16, 192, 2048], P('dp', 'expert'), may hold values from -0.125 to 0.125
- down_weight: bfloat16 [32, 16, 192, 2048], P('dp', 'expert'), may hold values from -0.21875 to 0.21875
Outputs:
- mixed: bfloat16 [32768, 2048], P(('dp', 'expert'))
The draws below stay inside these ranges and needn't reach their ends.
Inputs may be any that keep to these rules, and one draw needn't show every extreme that they name: `routes`: each token names 8 different experts. Among the tokens of one device no expert is named by more than 6 tokens, a bound that some block reaches.
All inputs are finite; a program needn't handle non-finite values.
Results may differ from the reference program's by a relative error of at most 0.0072.
Values may be sent and summed in bfloat16 or wider, within the bound.
No kernel may reach another device: no remote copies, remote signals or barrier semaphores. Data moves between devices by JAX's collectives and lax.ppermute only.
A program may use at most 128 MiB of HBM per device.

```python
import math
import jax
import jax.numpy as jnp
import numpy as np
from jax import lax

D = 2048
FF = 768
TOPK = 8
SPLIT = 4
TOK_DEV = 64
HID = 192
EXPERTS = 128
MOST = 6
TOKENS = 32768
N_DP = 32
N_EXPERT = 16
DEVICES = 512


def level_of(stream_key, shape, shards, least, high):
    def one(position, blocks):
        steps = jax.random.uniform(jax.random.fold_in(jax.random.fold_in(stream_key, 6), position), (blocks,), jnp.float32, least / len(shards), high / len(shards))
        return jnp.repeat(jnp.exp(steps), shape[position] // blocks).reshape((-1,) + (1,) * (len(shape) - position - 1))

    factor_of = one(*shards[0])
    for cut in shards[1:]:
        factor_of = factor_of * one(*cut)
    return factor_of


def shared_out(own_key, own, number, rows, amount, top, most, slope):
    order = jax.random.permutation(own_key, amount)
    crowded, ordinary = shares(amount, rows * top, most, slope, True), shares(amount, rows * top, most, slope, False)
    places = jnp.arange(amount)

    def named(lengths, offset_by):
        used = int((lengths > 0).sum())
        fixed = max(1, used // 4)
        moved = fixed + (places - fixed + offset_by * (used - fixed)) % max(1, amount - fixed)
        return jnp.zeros((amount,), jnp.int32).at[order[jnp.where(places < fixed, places, moved)]].set(jnp.asarray(lengths, jnp.int32))

    lengths = jnp.where(number % 4 == 0, named(crowded, number // 4), named(ordinary, number - number // 4 - 1))
    mixed = jax.random.permutation(jax.random.fold_in(own, 3), amount)
    donor, sink = mixed[0:amount // 2 * 2:2], mixed[1:amount // 2 * 2:2]
    slack = jnp.minimum(lengths[donor] - 1, most - lengths[sink]) // 2
    slack = jnp.where((donor == order[0]) | (sink == order[0]) | (lengths[sink] == 0), 0, jnp.maximum(slack, 0))
    moved = jax.random.randint(jax.random.fold_in(own, 4), (amount // 2,), 0, 1 << 20) % (slack + 1)
    lengths = lengths.at[donor].add(-moved).at[sink].add(moved)
    members = jnp.searchsorted(jnp.cumsum(lengths), jnp.arange(rows * top), side="right").astype(jnp.int32)
    grid = members.reshape(top, rows).T
    grid = grid[jax.random.permutation(jax.random.fold_in(own, 1), rows)]
    offset_by = jax.random.randint(jax.random.fold_in(own, 2), (rows, 1), 0, top)
    return jnp.take_along_axis(grid, (jnp.arange(top)[None, :] + offset_by) % top, axis=1)


def shares(number_of, total, limit, lean, full):
    weights = [(1 << 20) // math.isqrt(rank ** lean) + 1 for rank in range(1, number_of + 1)]
    largest = limit if full else min(limit, max(-(-total // number_of), total * weights[0] // sum(weights)))
    least = 1 if total - largest >= number_of - 1 else 0
    counts, surplus = [largest] + [least] * (number_of - 1), total - largest - least * (number_of - 1)
    while surplus > 0:
        movable = [i for i in range(1, number_of) if counts[i] < largest] or [i for i in range(1, number_of) if counts[i] < limit]
        pool, left = sum([weights[i] for i in movable]), surplus
        for i in movable:
            addition = min(limit - counts[i], max(1, left * weights[i] // pool), surplus)
            counts[i] = counts[i] + addition
            surplus = surplus - addition
    return np.array(counts)


def centred(own_key, dims, scale, limit, shards=(), kind=jnp.bfloat16):
    array = scale * jax.random.normal(own_key, dims, jnp.float32)
    if shards:
        array = array * level_of(own_key, dims, shards, -0.22, 0.18)
    return jnp.clip(array, -limit, limit).astype(kind)


def setup_inputs(seed: int = 0) -> dict:
    keys = jax.random.split(jax.random.key(seed), 7)
    tokens = centred(keys[0], (TOKENS, D), 1.0, 6.0, ((0, 512),))
    routes_keys = jax.random.split(jax.random.fold_in(keys[1], 1), TOKENS // TOK_DEV)
    routes_turns = jax.random.permutation(jax.random.fold_in(keys[1], 3), TOKENS // TOK_DEV)
    routes = jax.vmap(lambda own, number: shared_out(jax.random.fold_in(keys[1], 2), own, number, TOK_DEV, EXPERTS, TOPK, MOST, 2))(routes_keys, routes_turns).reshape((TOKENS, TOPK))
    route_weights = jnp.clip(jnp.exp(math.log(0.5) - 2.3025851 * jax.random.uniform(keys[2], (TOKENS, TOPK), jnp.float32) ** level_of(keys[2], (TOKENS, TOPK), ((0, 512),), -0.2, 0.2)), 0.05, 0.5)
    gate_weight = centred(keys[3], (N_DP, N_EXPERT, HID, D), D ** -0.5, 0.125, ((0, 32), (1, 16)))
    up_weight = centred(keys[4], (N_DP, N_EXPERT, HID, D), D ** -0.5, 0.125, ((0, 32), (1, 16)))
    down_weight = centred(keys[5], (N_DP, N_EXPERT, HID, D), FF ** -0.5, 0.21875, ((0, 32), (1, 16)))
    return {"tokens": tokens, "routes": routes, "route_weights": route_weights, "gate_weight": gate_weight, "up_weight": up_weight, "down_weight": down_weight}


def add_rounded(first, second):
    first, second = lax.optimization_barrier((first, second))
    return (first.astype(jnp.float32) + second.astype(jnp.float32)).astype(jnp.bfloat16)


def reference(tokens, routes, route_weights, gate_weight, up_weight, down_weight):
    group_count = N_DP // SPLIT
    cap_rows = DEVICES * MOST
    flat_ids = routes.reshape(-1)
    flat_weights = route_weights.reshape(-1)
    zero_index = jnp.int32(0)
    slot_positions = jnp.arange(cap_rows, dtype=jnp.int32)

    def one_expert(total, expert_id):
        column = (expert_id // group_count).astype(jnp.int32)
        first_row = ((expert_id % group_count) * SPLIT).astype(jnp.int32)
        gate_part = lax.dynamic_slice(gate_weight, (first_row, column, zero_index, zero_index), (SPLIT, 1, HID, D))
        up_part = lax.dynamic_slice(up_weight, (first_row, column, zero_index, zero_index), (SPLIT, 1, HID, D))
        down_part = lax.dynamic_slice(down_weight, (first_row, column, zero_index, zero_index), (SPLIT, 1, HID, D))
        gate_full = gate_part.reshape(FF, D).T
        up_full = up_part.reshape(FF, D).T
        down_full = down_part.reshape(FF, D)
        chosen = flat_ids == expert_id
        chosen_count = jnp.sum(chosen.astype(jnp.int32))
        picked_index = jnp.nonzero(chosen, size=cap_rows, fill_value=0)[0].astype(jnp.int32)
        valid = (slot_positions < chosen_count).astype(jnp.float32)
        token_index = (picked_index // TOPK).astype(jnp.int32)
        expert_rows = tokens[token_index]
        gate_value = jnp.dot(expert_rows, gate_full, preferred_element_type=jnp.float32)
        up_value = jnp.dot(expert_rows, up_full, preferred_element_type=jnp.float32)
        hidden = (jax.nn.silu(gate_value) * up_value).astype(jnp.bfloat16)
        parts = [jnp.dot(hidden[:, q * HID:(q + 1) * HID], down_full[q * HID:(q + 1) * HID], preferred_element_type=jnp.float32).astype(jnp.bfloat16) for q in range(SPLIT)]
        pair_low = add_rounded(parts[0], parts[2])
        pair_high = add_rounded(parts[1], parts[3])
        expert_out = add_rounded(pair_low, pair_high)
        scaled = expert_out.astype(jnp.float32) * (flat_weights[picked_index] * valid)[:, None]
        return total.at[token_index].add(scaled), None

    start_total = jnp.zeros((TOKENS, D), jnp.float32)
    total, unused = lax.scan(one_expert, start_total, jnp.arange(EXPERTS, dtype=jnp.int32))
    return total.astype(jnp.bfloat16)
```

```python
import jax
import jax.numpy as jnp
from jax import lax
from jax.experimental import pallas as pl
from jax.experimental.pallas import tpu as pltpu
from jax.sharding import Mesh, PartitionSpec as P

SIZES = (4, 2, 2, 2, 8, 2)
NAMES = ("x", "h", "p", "b", "z", "c")
MOST = 6
CHUNKS = 4
PLANE = 32
EXTRA = 128


def flips(axes):
    return [(i, i ^ (2 ** len(axes) - 1)) for i in range(2 ** len(axes))]


def place(p, b, c):
    return p * 4 + b * 2 + c


FIRST = [
    (place(1, 0, 0), place(0, 1, 1)),
    (place(1, 1, 0), place(0, 0, 1)),
    (place(0, 1, 1), place(1, 0, 0)),
    (place(0, 0, 1), place(1, 1, 0)),
    (place(0, 0, 0), place(0, 1, 0)),
    (place(0, 1, 0), place(0, 0, 0)),
    (place(1, 0, 1), place(1, 1, 1)),
    (place(1, 1, 1), place(1, 0, 1)),
]
SECOND = [
    (place(0, 0, 1), place(0, 1, 1)),
    (place(0, 1, 1), place(0, 0, 1)),
    (place(1, 0, 0), place(1, 1, 0)),
    (place(1, 1, 0), place(1, 0, 0)),
]
PARTNERS = (("p",), ("h", "p", "b"), ("h", "b"))


def swap(value, axes):
    return lax.ppermute(value, axes, flips(axes))


def expert_kernel(rows_ref, *refs):
    gates, ups, downs, out_ref = refs[0:4], refs[4:8], refs[8:12], refs[12]
    rows = rows_ref[...]
    total = None
    for gate, up, down in zip(gates, ups, downs):
        dims = (((1,), (1,)), ((), ()))
        g = lax.dot_general(rows, gate[...], dims, preferred_element_type=jnp.float32)
        u = lax.dot_general(rows, up[...], dims, preferred_element_type=jnp.float32)
        hidden = (g / (1.0 + jnp.exp(-g)) * u).astype(jnp.bfloat16)
        part = jnp.dot(hidden, down[...], preferred_element_type=jnp.float32)
        total = part if total is None else total + part
    out_ref[...] = total.astype(jnp.bfloat16)


def run_expert(rows, gates, ups, downs):
    count, width = rows.shape
    hid = gates[0].shape[0]
    tile = 256
    whole = pl.BlockSpec((hid, width), lambda i: (0, 0))
    block = pl.BlockSpec((tile, width), lambda i: (i, 0))
    return pl.pallas_call(
        expert_kernel,
        grid=(count // tile,),
        out_shape=jax.ShapeDtypeStruct((count, width), jnp.bfloat16),
        in_specs=[block] + [whole] * 12,
        out_specs=block,
        compiler_params=pltpu.CompilerParams(vmem_limit_bytes=48 * 1024 * 1024),
        cost_estimate=pl.CostEstimate(
            flops=2 * count * width * hid * 12,
            bytes_accessed=4 * count * width + 24 * hid * width,
            transcendentals=count * hid * 4,
        ),
    )(rows, *gates, *ups, *downs)


def shards(tokens, routes, route_weights, gate_weight, up_weight, down_weight):
    count, width = tokens.shape
    top = routes.shape[1]
    x, h, p, z, c = (lax.axis_index(n) for n in ("x", "h", "p", "z", "c"))

    high = route_weights.astype(jnp.bfloat16)
    low = (route_weights - high.astype(jnp.float32)).astype(jnp.bfloat16)
    fields = (routes.astype(jnp.bfloat16), high, low)
    meta = sum(
        jnp.pad(f, ((0, 0), (top * k, EXTRA - top * (k + 1)))) for k, f in enumerate(fields)
    )
    record = jnp.concatenate([tokens, meta], axis=1)
    records = [record] + [swap(record, axes) for axes in PARTNERS]

    own = [gate_weight[0, 0], up_weight[0, 0], down_weight[0, 0]]
    axes = ("p", "b", "c")
    first = [lax.ppermute(w, axes, FIRST) for w in own]
    second = [lax.ppermute(w, axes, SECOND) for w in first]
    second = [jnp.where(c == p, mine, got) for mine, got in zip(own, second)]
    third = [swap(w, ("c",)) for w in first]
    fourth = [swap(w, ("c",)) for w in second]
    pieces = [list(four) for four in zip(first, second, third, fourth)]

    held = jnp.concatenate(records, axis=0)
    rows = held[:, :width]
    meta = held[:, width:].astype(jnp.float32)
    named = meta[:, :top].astype(jnp.int32)
    weight = meta[:, top : 2 * top] + meta[:, 2 * top : 3 * top]
    target = jnp.arange(PLANE, dtype=jnp.int32)
    expert = (2 * (target % 8) + p) * 8 + 2 * (target // 8) + h
    match = named[:, :, None] == expert[None, None, :]
    chosen = jnp.any(match, axis=1)
    weight = jnp.sum(jnp.where(match, weight[:, :, None], 0.0), axis=1)
    order = jnp.arange(CHUNKS * count, dtype=jnp.int32)
    before = (order[:, None] // count == order[None, :] // count) & (order[None, :] < order[:, None])
    rank = jnp.dot(
        before.astype(jnp.bfloat16), chosen.astype(jnp.bfloat16), preferred_element_type=jnp.float32
    ).astype(jnp.int32)
    slot = jnp.where(chosen, rank + (order // count * MOST)[:, None], -1).T
    slots = jnp.arange(CHUNKS * MOST, dtype=jnp.int32)
    hit = (slot[:, None, :] == slots[None, :, None]).reshape(PLANE * CHUNKS * MOST, CHUNKS * count)
    outgoing = jnp.dot(
        hit.astype(jnp.bfloat16), rows, preferred_element_type=jnp.float32
    ).astype(jnp.bfloat16)
    share = (PLANE, CHUNKS * MOST, width)
    arrived = lax.all_to_all(outgoing.reshape(share), ("x", "z"), 0, 0, tiled=True)

    results = run_expert(arrived.reshape(-1, width), *pieces)

    returned = lax.all_to_all(results.reshape(share), ("x", "z"), 0, 0, tiled=True)
    returned = returned.reshape(-1, width)
    spread = jnp.broadcast_to(
        weight.T[:, None, :], (PLANE, CHUNKS * MOST, CHUNKS * count)
    ).reshape(hit.shape)
    spread = jnp.where(hit, spread, 0.0)
    upper = spread.astype(jnp.bfloat16)
    lower = (spread - upper.astype(jnp.float32)).astype(jnp.bfloat16)
    dims = (((0,), (0,)), ((), ()))
    partial = lax.dot_general(
        upper, returned, dims, preferred_element_type=jnp.float32
    ) + lax.dot_general(lower, returned, dims, preferred_element_type=jnp.float32)
    mixed = partial[:count]
    for k, names in enumerate(PARTNERS, 1):
        sent = partial[k * count : (k + 1) * count].astype(jnp.bfloat16)
        mixed = mixed + swap(sent, names).astype(jnp.float32)
    return mixed.astype(jnp.bfloat16)


def solution(mesh):
    fine = Mesh(mesh.devices.reshape(SIZES), NAMES)
    rows = P(NAMES, None)
    weights = P(("x", "h", "p", "b"), ("z", "c"), None, None)
    return jax.shard_map(
        shards,
        mesh=fine,
        in_specs=(rows, rows, rows, weights, weights, weights),
        out_specs=rows,
        check_vma=False,
    )
```

```python
import jax
import jax.numpy as jnp
from jax import lax
from jax.experimental import pallas as pl
from jax.experimental.pallas import tpu as pltpu
from jax.sharding import Mesh, PartitionSpec as P

SIZES = (4, 2, 2, 2, 8, 2)
NAMES = ("x", "h", "p", "b", "z", "c")
MOST = 6
CHUNKS = 4
PLANE = 32
EXTRA = 128
LANES = 128


def flips(axes):
    return [(i, i ^ (2 ** len(axes) - 1)) for i in range(2 ** len(axes))]


def place(p, b, c):
    return p * 4 + b * 2 + c


FIRST = [
    (place(1, 0, 0), place(0, 1, 1)),
    (place(1, 1, 0), place(0, 0, 1)),
    (place(0, 1, 1), place(1, 0, 0)),
    (place(0, 0, 1), place(1, 1, 0)),
    (place(0, 0, 0), place(0, 1, 0)),
    (place(0, 1, 0), place(0, 0, 0)),
    (place(1, 0, 1), place(1, 1, 1)),
    (place(1, 1, 1), place(1, 0, 1)),
]
SECOND = [
    (place(0, 0, 1), place(0, 1, 1)),
    (place(0, 1, 1), place(0, 0, 1)),
    (place(1, 0, 0), place(1, 1, 0)),
    (place(1, 1, 0), place(1, 0, 0)),
]
PARTNERS = (("p",), ("h", "p", "b"), ("h", "b"))


def swap(value, axes):
    return lax.ppermute(value, axes, flips(axes))


def expert_kernel(group_ref, rows_ref, *refs):
    pieces, out_ref = refs[:12], refs[12]
    gate, up, down, lined, sems = refs[13:]
    first = pl.program_id(0) == 0
    hid = pieces[0].shape[0]
    copies = [
        pltpu.make_async_copy(piece, into.at[pl.ds(k % 4 * hid, hid)], sems.at[k])
        for k, (piece, into) in enumerate(zip(pieces, [gate] * 4 + [up] * 4 + [down] * 4))
    ]

    @pl.when(first)
    def _():
        for copy in copies:
            copy.start()
        for copy in copies[:8]:
            copy.wait()

    dims = (((1,), (1,)), ((), ()))
    rows = rows_ref[...]
    g = lax.dot_general(rows, gate[...], dims, preferred_element_type=jnp.float32)
    u = lax.dot_general(rows, up[...], dims, preferred_element_type=jnp.float32)
    hidden = (g / (1.0 + jnp.exp(-g)) * u).astype(jnp.bfloat16)

    @pl.when(first)
    def _():
        for copy in copies[8:]:
            copy.wait()

    result = jnp.dot(hidden, down[...], preferred_element_type=jnp.float32)
    count = rows.shape[0]
    lines = result.shape[1] // LANES
    for k in range(lines):
        lined[pl.ds(k, count, stride=lines), :] = result[:, k * LANES : (k + 1) * LANES]
    block = MOST * lines
    for k in range(count // MOST):
        z, m = divmod(k, CHUNKS)
        out_ref[0, m ^ group_ref[0], z] = lined[k * block : (k + 1) * block, :].astype(jnp.bfloat16)


def run_expert(group, rows, pieces):
    count, width = rows.shape
    hid = pieces[0].shape[0]
    xs, zs = SIZES[0], SIZES[4]
    tile = count // xs
    lines = width // LANES
    shape = (CHUNKS, zs, MOST * lines, LANES)
    return pl.pallas_call(
        expert_kernel,
        grid=(xs,),
        out_shape=jax.ShapeDtypeStruct((xs,) + shape, jnp.bfloat16),
        in_specs=[
            pl.BlockSpec(memory_space=pltpu.SMEM),
            pl.BlockSpec((tile, width), lambda i: (i, 0)),
        ]
        + [pl.BlockSpec(memory_space=pl.ANY)] * 12,
        out_specs=pl.BlockSpec((1,) + shape, lambda i: (i, 0, 0, 0, 0)),
        scratch_shapes=[pltpu.VMEM((4 * hid, width), jnp.bfloat16)] * 3
        + [pltpu.VMEM((tile * lines, LANES), jnp.float32), pltpu.SemaphoreType.DMA((12,))],
        compiler_params=pltpu.CompilerParams(vmem_limit_bytes=28 * 1024 * 1024),
        cost_estimate=pl.CostEstimate(
            flops=2 * count * width * hid * 12,
            bytes_accessed=4 * count * width + 24 * hid * width,
            transcendentals=count * hid * 4,
        ),
    )(group, rows, *pieces)


def member_groups():
    def index(x, member, z, kind, c):
        h = member >> 1
        at = x
        for n, coordinate in zip(SIZES[1:], (h, (member & 1) ^ h, kind ^ h, z, c)):
            at = at * n + coordinate
        return at

    return [
        [
            index(x, member, z, kind, c)
            for x in range(SIZES[0])
            for member in range(CHUNKS)
            for z in range(SIZES[4])
        ]
        for kind in range(2)
        for c in range(2)
    ]


def matches(named, experts):
    return named[:, :, None] == experts[None, None, :]


def ranks(chosen, count):
    order = jnp.arange(chosen.shape[0], dtype=jnp.int32)
    before = (order[:, None] // count == order[None, :] // count) & (order[None, :] < order[:, None])
    return jnp.dot(
        before.astype(jnp.bfloat16), chosen.astype(jnp.bfloat16), preferred_element_type=jnp.float32
    ).astype(jnp.int32)


def shards(tokens, routes, route_weights, gate_weight, up_weight, down_weight):
    count, width = tokens.shape
    top = routes.shape[1]
    h, p, c = (lax.axis_index(n) for n in ("h", "p", "c"))
    xs, zs = SIZES[0], SIZES[4]

    meta = jnp.pad(routes.astype(jnp.bfloat16), ((0, 0), (0, EXTRA - top)))
    record = jnp.concatenate([tokens, meta], axis=1)
    records = jnp.concatenate([record] + [swap(record, axes) for axes in PARTNERS], axis=0)

    own = [gate_weight[0, 0], up_weight[0, 0], down_weight[0, 0]]
    axes = ("p", "b", "c")
    first = [lax.ppermute(w, axes, FIRST) for w in own]

    named = records[:, width : width + top].astype(jnp.int32)
    target = jnp.arange(PLANE, dtype=jnp.int32)
    chosen = jnp.any(matches(named, (2 * (target % zs) + p) * 8 + 2 * (target // zs) + h), axis=1)
    chunk = jnp.arange(CHUNKS * count, dtype=jnp.int32) // count
    slot = jnp.where(chosen, ranks(chosen, count) + (chunk * MOST)[:, None], -1).T
    slots = jnp.arange(CHUNKS * MOST, dtype=jnp.int32)
    hit = (slot[:, None, :] == slots[None, :, None]).reshape(PLANE * CHUNKS * MOST, CHUNKS * count)
    sent = jnp.dot(
        hit.astype(jnp.bfloat16), records[:, :width], preferred_element_type=jnp.float32
    ).astype(jnp.bfloat16)
    sent, first[0] = lax.optimization_barrier((sent, first[0]))
    arrived = lax.all_to_all(
        sent.reshape(PLANE, CHUNKS * MOST, width), ("x", "z"), 0, 0, tiled=True
    )

    second = [lax.ppermute(w, axes, SECOND) for w in first]
    second = [jnp.where(c == p, mine, got) for mine, got in zip(own, second)]
    third = [swap(w, ("c",)) for w in first]
    fourth = [swap(w, ("c",)) for w in second]
    pieces = [piece for four in zip(first, second, third, fourth) for piece in four]

    group = (2 * h + (p ^ h)).astype(jnp.int32).reshape(1)
    results = run_expert(group, arrived.reshape(-1, width), pieces)

    returned = lax.all_to_all(
        results.reshape((xs * CHUNKS * zs,) + results.shape[3:]),
        NAMES,
        0,
        0,
        axis_index_groups=member_groups(),
        tiled=True,
    )
    returned = returned.reshape(-1, width)

    target = jnp.arange(xs * CHUNKS * zs, dtype=jnp.int32)
    half = target // zs % CHUNKS // 2
    column = 2 * (target % zs) + (target // zs % 2 ^ half)
    match = matches(routes, column * 8 + 2 * (target // (zs * CHUNKS)) + half)
    chosen = jnp.any(match, axis=1)
    weight = jnp.sum(jnp.where(match, route_weights[:, :, None], 0.0), axis=1)
    slot = jnp.where(chosen, ranks(chosen, count), -1).T
    slots = jnp.arange(MOST, dtype=jnp.int32)
    spread = jnp.where(slot[:, None, :] == slots[None, :, None], weight.T[:, None, :], 0.0)
    spread = spread.reshape(-1, count)
    upper = spread.astype(jnp.bfloat16)
    lower = (spread - upper.astype(jnp.float32)).astype(jnp.bfloat16)
    dims = (((0,), (0,)), ((), ()))
    mixed = lax.dot_general(
        upper, returned, dims, preferred_element_type=jnp.float32
    ) + lax.dot_general(lower, returned, dims, preferred_element_type=jnp.float32)
    return mixed.astype(jnp.bfloat16)


def solution(mesh):
    fine = Mesh(mesh.devices.reshape(SIZES), NAMES)
    rows = P(NAMES, None)
    weights = P(("x", "h", "p", "b"), ("z", "c"), None, None)
    return jax.shard_map(
        shards,
        mesh=fine,
        in_specs=(rows, rows, rows, weights, weights, weights),
        out_specs=rows,
        check_vma=False,
    )
```

```python
import jax
import jax.numpy as jnp
from jax import lax
from jax.experimental import pallas as pl
from jax.experimental.pallas import tpu as pltpu
from jax.sharding import Mesh, PartitionSpec as P

SIZES = (4, 2, 2, 2, 8, 2)
NAMES = ("x", "h", "p", "b", "z", "c")
MOST = 6
CHUNKS = 4
PLANE = 32
EXTRA = 128
SPLIT = 4


def flips(axes):
    return [(i, i ^ (2 ** len(axes) - 1)) for i in range(2 ** len(axes))]


def place(p, b, c):
    return p * 4 + b * 2 + c


FIRST = [
    (place(1, 0, 0), place(0, 1, 1)),
    (place(1, 1, 0), place(0, 0, 1)),
    (place(0, 1, 1), place(1, 0, 0)),
    (place(0, 0, 1), place(1, 1, 0)),
    (place(0, 0, 0), place(0, 1, 0)),
    (place(0, 1, 0), place(0, 0, 0)),
    (place(1, 0, 1), place(1, 1, 1)),
    (place(1, 1, 1), place(1, 0, 1)),
]
SECOND = [
    (place(0, 0, 1), place(0, 1, 1)),
    (place(0, 1, 1), place(0, 0, 1)),
    (place(1, 0, 0), place(1, 1, 0)),
    (place(1, 1, 0), place(1, 0, 0)),
]
PARTNERS = (("p",), ("h", "p", "b"), ("h", "b"))


def swap(value, axes):
    return lax.ppermute(value, axes, flips(axes))


def expert_kernel(rows_ref, *refs):
    pieces, out_ref = refs[:4], refs[4]
    panels, sems = refs[5:8], refs[8]
    first = pl.program_id(0) == 0
    hid = pieces[0].shape[0] // 3
    copies = [
        pltpu.make_async_copy(
            piece.at[pl.ds(k * hid, hid)], panel.at[pl.ds(q * hid, hid)], sems.at[k * SPLIT + q]
        )
        for k, panel in enumerate(panels)
        for q, piece in enumerate(pieces)
    ]

    @pl.when(first)
    def _():
        for copy in copies:
            copy.start()
        for copy in copies[: 2 * SPLIT]:
            copy.wait()

    gate, up, down = panels
    dims = (((1,), (1,)), ((), ()))
    rows = rows_ref[...]
    g = lax.dot_general(rows, gate[...], dims, preferred_element_type=jnp.float32)
    u = lax.dot_general(rows, up[...], dims, preferred_element_type=jnp.float32)
    hidden = (g / (1.0 + jnp.exp(-g)) * u).astype(jnp.bfloat16)

    @pl.when(first)
    def _():
        for copy in copies[2 * SPLIT :]:
            copy.wait()

    out_ref[...] = jnp.dot(hidden, down[...], preferred_element_type=jnp.float32).astype(
        jnp.bfloat16
    )


def run_expert(rows, pieces):
    count, width = rows.shape
    hid = pieces[0].shape[0] // 3
    tile = 256
    block = pl.BlockSpec((tile, width), lambda i: (i, 0))
    return pl.pallas_call(
        expert_kernel,
        grid=(count // tile,),
        out_shape=jax.ShapeDtypeStruct((count, width), jnp.bfloat16),
        in_specs=[block] + [pl.BlockSpec(memory_space=pltpu.HBM)] * SPLIT,
        out_specs=block,
        scratch_shapes=[pltpu.VMEM((SPLIT * hid, width), jnp.bfloat16)] * 3
        + [pltpu.SemaphoreType.DMA((3 * SPLIT,))],
        compiler_params=pltpu.CompilerParams(vmem_limit_bytes=60 * 1024 * 1024),
        cost_estimate=pl.CostEstimate(
            flops=2 * count * width * hid * 12,
            bytes_accessed=4 * count * width + 24 * hid * width,
            transcendentals=count * hid * 4,
        ),
    )(rows, *pieces)


def pick_kernel(hit_ref, *refs):
    sources, out_ref = refs[:-1], refs[-1]
    count = sources[0].shape[0]
    total = None
    for k, source in enumerate(sources):
        part = jnp.dot(
            hit_ref[:, k * count : (k + 1) * count], source[...], preferred_element_type=jnp.float32
        )
        total = part if total is None else total + part
    out_ref[...] = total.astype(jnp.bfloat16)


def pick_rows(hit, sources, width):
    count, tokens = hit.shape
    tile = 256
    whole = pl.BlockSpec((tokens // len(sources), width), lambda i: (0, 0))
    return pl.pallas_call(
        pick_kernel,
        grid=(count // tile,),
        out_shape=jax.ShapeDtypeStruct((count, width), jnp.bfloat16),
        in_specs=[pl.BlockSpec((tile, tokens), lambda i: (i, 0))] + [whole] * len(sources),
        out_specs=pl.BlockSpec((tile, width), lambda i: (i, 0)),
        compiler_params=pltpu.CompilerParams(vmem_limit_bytes=16 * 1024 * 1024),
        cost_estimate=pl.CostEstimate(
            flops=2 * count * tokens * width,
            bytes_accessed=2 * (count + tokens) * (width + tokens),
            transcendentals=0,
        ),
    )(hit, *sources)


def matches(named, experts):
    return named[:, :, None] == experts[None, None, :]


def ranks(chosen, count):
    order = jnp.arange(chosen.shape[0], dtype=jnp.int32)
    before = (order[:, None] // count == order[None, :] // count) & (order[None, :] < order[:, None])
    return jnp.dot(
        before.astype(jnp.bfloat16), chosen.astype(jnp.bfloat16), preferred_element_type=jnp.float32
    ).astype(jnp.int32)


def shards(tokens, routes, route_weights, gate_weight, up_weight, down_weight):
    count, width = tokens.shape
    top = routes.shape[1]
    h, p, c = (lax.axis_index(n) for n in ("h", "p", "c"))
    zs = SIZES[4]

    high = route_weights.astype(jnp.bfloat16)
    low = (route_weights - high.astype(jnp.float32)).astype(jnp.bfloat16)
    fields = (routes.astype(jnp.bfloat16), high, low)
    meta = sum(
        jnp.pad(f, ((0, 0), (top * k, EXTRA - top * (k + 1)))) for k, f in enumerate(fields)
    )
    record = jnp.concatenate([tokens, meta], axis=1)
    received = [swap(record, axes) for axes in PARTNERS]

    own = jnp.concatenate([gate_weight[0, 0], up_weight[0, 0], down_weight[0, 0]], axis=0)
    own, received = lax.optimization_barrier((own, received))
    axes = ("p", "b", "c")
    first = lax.ppermute(own, axes, FIRST)
    second = jnp.where(c == p, own, lax.ppermute(first, axes, SECOND))
    pieces = [first, second, swap(first, ("c",)), swap(second, ("c",))]

    records = [record] + received
    meta = jnp.concatenate([r[:, width:] for r in records], axis=0).astype(jnp.float32)
    named = meta[:, :top].astype(jnp.int32)
    weight = meta[:, top : 2 * top] + meta[:, 2 * top : 3 * top]
    target = jnp.arange(PLANE, dtype=jnp.int32)
    match = matches(named, (2 * (target % zs) + p) * 8 + 2 * (target // zs) + h)
    chosen = jnp.any(match, axis=1)
    weight = jnp.sum(jnp.where(match, weight[:, :, None], 0.0), axis=1)
    chunk = jnp.arange(CHUNKS * count, dtype=jnp.int32) // count
    slot = jnp.where(chosen, ranks(chosen, count) + (chunk * MOST)[:, None], -1).T
    slots = jnp.arange(CHUNKS * MOST, dtype=jnp.int32)
    hit = (slot[:, None, :] == slots[None, :, None]).reshape(PLANE * CHUNKS * MOST, CHUNKS * count)
    spread = jnp.broadcast_to(
        weight.T[:, None, :], (PLANE, CHUNKS * MOST, CHUNKS * count)
    ).reshape(hit.shape)
    spread = jnp.where(hit, spread, 0.0)
    upper = spread.astype(jnp.bfloat16)
    lower = (spread - upper.astype(jnp.float32)).astype(jnp.bfloat16)

    def exchange(rows):
        share = (PLANE, CHUNKS * MOST, width)
        return lax.all_to_all(rows.reshape(share), ("x", "z"), 0, 0, tiled=True).reshape(-1, width)

    sent = pick_rows(hit.astype(jnp.bfloat16), records, width)
    returned = exchange(run_expert(exchange(sent), pieces))

    dims = (((0,), (0,)), ((), ()))
    partial = lax.dot_general(
        upper, returned, dims, preferred_element_type=jnp.float32
    ) + lax.dot_general(lower, returned, dims, preferred_element_type=jnp.float32)
    mixed = partial[:count]
    for k, names in enumerate(PARTNERS, 1):
        part = partial[k * count : (k + 1) * count].astype(jnp.bfloat16)
        mixed = mixed + swap(part, names).astype(jnp.float32)
    return mixed.astype(jnp.bfloat16)


def solution(mesh):
    fine = Mesh(mesh.devices.reshape(SIZES), NAMES)
    rows = P(NAMES, None)
    weights = P(("x", "h", "p", "b"), ("z", "c"), None, None)
    return jax.shard_map(
        shards,
        mesh=fine,
        in_specs=(rows, rows, rows, weights, weights, weights),
        out_specs=rows,
        check_vma=False,
    )
```

```python
import jax
import jax.numpy as jnp
from jax import lax
from jax.experimental import pallas as pl
from jax.experimental.pallas import tpu as pltpu
from jax.sharding import Mesh, PartitionSpec as P

SIZES = (4, 2, 2, 2, 8, 2)
NAMES = ("x", "h", "p", "b", "z", "c")
MOST = 6
CHUNKS = 4
PLANE = 32
EXTRA = 128
LANES = 128
WIDE = 256
SPLIT = 4


def flips(axes):
    return [(i, i ^ (2 ** len(axes) - 1)) for i in range(2 ** len(axes))]


def place(p, b, c):
    return p * 4 + b * 2 + c


FIRST = [
    (place(1, 0, 0), place(0, 1, 1)),
    (place(1, 1, 0), place(0, 0, 1)),
    (place(0, 1, 1), place(1, 0, 0)),
    (place(0, 0, 1), place(1, 1, 0)),
    (place(0, 0, 0), place(0, 1, 0)),
    (place(0, 1, 0), place(0, 0, 0)),
    (place(1, 0, 1), place(1, 1, 1)),
    (place(1, 1, 1), place(1, 0, 1)),
]
SECOND = [
    (place(0, 0, 1), place(0, 1, 1)),
    (place(0, 1, 1), place(0, 0, 1)),
    (place(1, 0, 0), place(1, 1, 0)),
    (place(1, 1, 0), place(1, 0, 0)),
]
PARTNERS = (("p",), ("h", "p", "b"), ("h", "b"))


def swap(value, axes):
    return lax.ppermute(value, axes, flips(axes))


def expert_kernel(rows_ref, *refs):
    pieces, (own_out, far_out) = refs[:SPLIT], refs[SPLIT : SPLIT + 2]
    panels, (hidden, lined, staged, in_sems, out_sems) = refs[6:9], refs[9:]
    hid = pieces[0].shape[0] // 3
    copies = [
        [
            pltpu.make_async_copy(
                piece.at[pl.ds(k * hid, hid)],
                panel.at[pl.ds(q * hid, hid)],
                in_sems.at[k * SPLIT + q],
            )
            for q, piece in enumerate(pieces)
        ]
        for k, panel in enumerate(panels)
    ]
    gates, ups, downs = copies
    for gate_copy, up_copy in zip(gates, ups):
        gate_copy.start()
        up_copy.start()
    for copy in downs:
        copy.start()

    gate, up, down = panels
    dims = (((1,), (1,)), ((), ()))
    rows = rows_ref[...]
    here = 0
    for start in range(0, SPLIT * hid, WIDE):
        while here * hid < start + WIDE:
            gates[here].wait()
            ups[here].wait()
            here += 1
        part = slice(start, start + WIDE)
        g = lax.dot_general(rows, gate[part, :], dims, preferred_element_type=jnp.float32)
        u = lax.dot_general(rows, up[part, :], dims, preferred_element_type=jnp.float32)
        hidden[:, part] = (g / (1.0 + jnp.exp(-g)) * u).astype(jnp.bfloat16)
    for copy in downs:
        copy.wait()

    lines = down.shape[1] // LANES
    tile = lined.shape[0] // lines
    share = CHUNKS * MOST
    sources = tile // share
    writes = []
    for k in range(rows.shape[0] // tile):
        result = jnp.dot(
            hidden[k * tile : (k + 1) * tile, :], down[...], preferred_element_type=jnp.float32
        )
        for n in range(lines):
            lined[pl.ds(n, tile, stride=lines), :] = result[:, n * LANES : (n + 1) * LANES]
        span = slice(k * sources, (k + 1) * sources)
        staged[span] = lined[...].astype(jnp.bfloat16).reshape(sources, share * lines, LANES)
        span = pl.ds(k * sources, sources)
        cut = MOST * lines
        for n, (out, part) in enumerate(
            ((own_out, pl.ds(0, cut)), (far_out, pl.ds(cut, share * lines - cut)))
        ):
            write = pltpu.make_async_copy(
                staged.at[span, part], out.at[span], out_sems.at[2 * k + n]
            )
            write.start()
            writes.append(write)
    for write in writes:
        write.wait()


def run_expert(rows, pieces):
    count, width = rows.shape
    hid = pieces[0].shape[0] // 3
    lines = width // LANES
    tile = count // 2
    cut = MOST * lines
    everything = (PLANE, CHUNKS * cut, LANES)
    return pl.pallas_call(
        expert_kernel,
        out_shape=[
            jax.ShapeDtypeStruct((PLANE, n, LANES), jnp.bfloat16) for n in (cut, (CHUNKS - 1) * cut)
        ],
        in_specs=[pl.BlockSpec(memory_space=pltpu.VMEM)]
        + [pl.BlockSpec(memory_space=pl.ANY)] * SPLIT,
        out_specs=[pl.BlockSpec(memory_space=pltpu.HBM)] * 2,
        scratch_shapes=[pltpu.VMEM((SPLIT * hid, width), jnp.bfloat16)] * 3
        + [
            pltpu.VMEM((count, SPLIT * hid), jnp.bfloat16),
            pltpu.VMEM((tile * lines, LANES), jnp.float32),
            pltpu.VMEM(everything, jnp.bfloat16),
            pltpu.SemaphoreType.DMA((3 * SPLIT,)),
            pltpu.SemaphoreType.DMA((2 * count // tile,)),
        ],
        compiler_params=pltpu.CompilerParams(vmem_limit_bytes=57 * 1024 * 1024),
        cost_estimate=pl.CostEstimate(
            flops=2 * count * width * hid * 12,
            bytes_accessed=4 * count * width + 24 * hid * width,
            transcendentals=count * hid * 4,
        ),
    )(rows, *pieces)


def pick_kernel(hit_ref, *refs):
    sources, out_ref = refs[:-1], refs[-1]
    rows = jnp.concatenate([source[...] for source in sources], axis=0)
    out_ref[...] = jnp.dot(hit_ref[...], rows, preferred_element_type=jnp.float32).astype(
        jnp.bfloat16
    )


def pick_rows(hit, sources, width):
    count, tokens = hit.shape
    tile = 256
    whole = pl.BlockSpec((tokens // len(sources), width), lambda i: (0, 0))
    return pl.pallas_call(
        pick_kernel,
        grid=(count // tile,),
        out_shape=jax.ShapeDtypeStruct((count, width), jnp.bfloat16),
        in_specs=[pl.BlockSpec((tile, tokens), lambda i: (i, 0))] + [whole] * len(sources),
        out_specs=pl.BlockSpec((tile, width), lambda i: (i, 0)),
        compiler_params=pltpu.CompilerParams(vmem_limit_bytes=16 * 1024 * 1024),
        cost_estimate=pl.CostEstimate(
            flops=2 * count * tokens * width,
            bytes_accessed=2 * (count + tokens) * (width + tokens),
            transcendentals=0,
        ),
    )(hit, *sources)


def matches(named, experts):
    return named[:, :, None] == experts[None, None, :]


def ranks(chosen, count):
    order = jnp.arange(chosen.shape[0], dtype=jnp.int32)
    before = (order[:, None] // count == order[None, :] // count) & (order[None, :] < order[:, None])
    return jnp.dot(
        before.astype(jnp.bfloat16), chosen.astype(jnp.bfloat16), preferred_element_type=jnp.float32
    ).astype(jnp.int32)


def shards(tokens, routes, route_weights, gate_weight, up_weight, down_weight):
    count, width = tokens.shape
    top = routes.shape[1]
    h, p, c = (lax.axis_index(n) for n in ("h", "p", "c"))
    zs = SIZES[4]

    high = route_weights.astype(jnp.bfloat16)
    low = (route_weights - high.astype(jnp.float32)).astype(jnp.bfloat16)
    fields = (routes.astype(jnp.bfloat16), high, low)
    meta = sum(
        jnp.pad(f, ((0, 0), (top * k, EXTRA - top * (k + 1)))) for k, f in enumerate(fields)
    )
    record = jnp.concatenate([tokens, meta], axis=1)
    received = [swap(record, axes) for axes in PARTNERS]

    own = jnp.concatenate([gate_weight[0, 0], up_weight[0, 0], down_weight[0, 0]], axis=0)
    own, received = lax.optimization_barrier((own, received))
    axes = ("p", "b", "c")
    first = lax.ppermute(own, axes, FIRST)
    second = jnp.where(c == p, own, lax.ppermute(first, axes, SECOND))
    pieces = [first, second, swap(first, ("c",)), swap(second, ("c",))]

    records = [record] + received
    meta = jnp.concatenate([r[:, width:] for r in records], axis=0).astype(jnp.float32)
    named = meta[:, :top].astype(jnp.int32)
    weight = meta[:, top : 2 * top] + meta[:, 2 * top : 3 * top]
    target = jnp.arange(PLANE, dtype=jnp.int32)
    match = matches(named, (2 * (target % zs) + p) * 8 + 2 * (target // zs) + h)
    chosen = jnp.any(match, axis=1)
    weight = jnp.sum(jnp.where(match, weight[:, :, None], 0.0), axis=1)
    chunk = jnp.arange(CHUNKS * count, dtype=jnp.int32) // count
    slot = jnp.where(chosen, ranks(chosen, count) + (chunk * MOST)[:, None], -1).T
    slots = jnp.arange(CHUNKS * MOST, dtype=jnp.int32)
    hit = (slot[:, None, :] == slots[None, :, None]).reshape(PLANE * CHUNKS * MOST, CHUNKS * count)
    sent = pick_rows(hit.astype(jnp.bfloat16), records, width)

    def exchange(rows):
        return lax.all_to_all(rows, ("x", "z"), 0, 0, tiled=True)

    arrived = exchange(sent.reshape(PLANE, CHUNKS * MOST, width)).reshape(-1, width)
    own_out, far_out = run_expert(arrived, pieces)

    spread = jnp.where(
        slot[:, None, :] == slots[None, :, None], weight.T[:, None, :], 0.0
    )
    upper = spread.astype(jnp.bfloat16)
    lower = (spread - upper.astype(jnp.float32)).astype(jnp.bfloat16)
    halves = [
        [
            half[:, :MOST, :count].reshape(-1, count),
            half[:, MOST:, count:].reshape(-1, (CHUNKS - 1) * count),
        ]
        for half in (upper, lower)
    ]
    halves, own_out = lax.optimization_barrier((halves, own_out))

    def combine(returned, k):
        returned = returned.reshape(-1, width)
        dims = (((0,), (0,)), ((), ()))
        return lax.dot_general(
            halves[0][k], returned, dims, preferred_element_type=jnp.float32
        ) + lax.dot_general(halves[1][k], returned, dims, preferred_element_type=jnp.float32)

    far_back = exchange(far_out)
    own_out, far_back = lax.optimization_barrier((own_out, far_back))
    own_back = exchange(own_out)
    far = combine(far_back, 1).astype(jnp.bfloat16)
    gained = [
        swap(far[k * count : (k + 1) * count], names) for k, names in enumerate(PARTNERS)
    ]
    mixed = combine(own_back, 0)
    for part in gained:
        mixed = mixed + part.astype(jnp.float32)
    return mixed.astype(jnp.bfloat16)


def solution(mesh):
    fine = Mesh(mesh.devices.reshape(SIZES), NAMES)
    rows = P(NAMES, None)
    weights = P(("x", "h", "p", "b"), ("z", "c"), None, None)
    return jax.shard_map(
        shards,
        mesh=fine,
        in_specs=(rows, rows, rows, weights, weights, weights),
        out_specs=rows,
        check_vma=False,
    )
```

```python
import jax
import jax.numpy as jnp
from jax import lax
from jax.experimental import pallas as pl
from jax.experimental.pallas import tpu as pltpu
from jax.sharding import Mesh, PartitionSpec as P

SIZES = (4, 2, 2, 2, 8, 2)
NAMES = ("x", "h", "p", "b", "z", "c")
MOST = 6
CHUNKS = 4
PLANE = 32
EXTRA = 128
LANES = 128
WIDE = 256
TOP = 8
SPLIT = 4


def flips(axes):
    return [(i, i ^ (2 ** len(axes) - 1)) for i in range(2 ** len(axes))]


def place(p, b, c):
    return p * 4 + b * 2 + c


FIRST = [
    (place(1, 0, 0), place(0, 1, 1)),
    (place(1, 1, 0), place(0, 0, 1)),
    (place(0, 1, 1), place(1, 0, 0)),
    (place(0, 0, 1), place(1, 1, 0)),
    (place(0, 0, 0), place(0, 1, 0)),
    (place(0, 1, 0), place(0, 0, 0)),
    (place(1, 0, 1), place(1, 1, 1)),
    (place(1, 1, 1), place(1, 0, 1)),
]
SECOND = [
    (place(0, 0, 1), place(0, 1, 1)),
    (place(0, 1, 1), place(0, 0, 1)),
    (place(1, 0, 0), place(1, 1, 0)),
    (place(1, 1, 0), place(1, 0, 0)),
]
PARTNERS = (("p",), ("h", "p", "b"), ("h", "b"))


def swap(value, axes):
    return lax.ppermute(value, axes, flips(axes))


def expert_kernel(rows_ref, *refs):
    pieces, (own_out, far_out) = refs[:SPLIT], refs[SPLIT : SPLIT + 2]
    panels, (hidden, lined, staged, in_sems, out_sems) = refs[6:9], refs[9:]
    hid = pieces[0].shape[0] // 3
    copies = [
        [
            pltpu.make_async_copy(
                piece.at[pl.ds(k * hid, hid)],
                panel.at[pl.ds(q * hid, hid)],
                in_sems.at[k * SPLIT + q],
            )
            for q, piece in enumerate(pieces)
        ]
        for k, panel in enumerate(panels)
    ]
    gates, ups, downs = copies
    for gate_copy, up_copy in zip(gates, ups):
        gate_copy.start()
        up_copy.start()
    for copy in downs:
        copy.start()

    gate, up, down = panels
    dims = (((1,), (1,)), ((), ()))
    rows = rows_ref[...]
    here = 0
    for start in range(0, SPLIT * hid, WIDE):
        while here * hid < start + WIDE:
            gates[here].wait()
            ups[here].wait()
            here += 1
        part = slice(start, start + WIDE)
        g = lax.dot_general(rows, gate[part, :], dims, preferred_element_type=jnp.float32)
        u = lax.dot_general(rows, up[part, :], dims, preferred_element_type=jnp.float32)
        hidden[:, part] = (g / (1.0 + jnp.exp(-g)) * u).astype(jnp.bfloat16)
    for copy in downs:
        copy.wait()

    lines = down.shape[1] // LANES
    tile = lined.shape[0] // lines
    share = CHUNKS * MOST
    sources = tile // share
    writes = []
    for k in range(rows.shape[0] // tile):
        result = jnp.dot(
            hidden[k * tile : (k + 1) * tile, :], down[...], preferred_element_type=jnp.float32
        )
        for n in range(lines):
            lined[pl.ds(n, tile, stride=lines), :] = result[:, n * LANES : (n + 1) * LANES]
        span = slice(k * sources, (k + 1) * sources)
        staged[span] = lined[...].astype(jnp.bfloat16).reshape(sources, share * lines, LANES)
        span = pl.ds(k * sources, sources)
        cut = MOST * lines
        for n, (out, part) in enumerate(
            ((own_out, pl.ds(0, cut)), (far_out, pl.ds(cut, share * lines - cut)))
        ):
            write = pltpu.make_async_copy(
                staged.at[span, part], out.at[span], out_sems.at[2 * k + n]
            )
            write.start()
            writes.append(write)
    for write in writes:
        write.wait()


def run_expert(rows, pieces):
    count, width = rows.shape
    hid = pieces[0].shape[0] // 3
    lines = width // LANES
    tile = count // 2
    cut = MOST * lines
    everything = (PLANE, CHUNKS * cut, LANES)
    return pl.pallas_call(
        expert_kernel,
        out_shape=[
            jax.ShapeDtypeStruct((PLANE, n, LANES), jnp.bfloat16) for n in (cut, (CHUNKS - 1) * cut)
        ],
        in_specs=[pl.BlockSpec(memory_space=pltpu.VMEM)]
        + [pl.BlockSpec(memory_space=pl.ANY)] * SPLIT,
        out_specs=[pl.BlockSpec(memory_space=pltpu.HBM)] * 2,
        scratch_shapes=[pltpu.VMEM((SPLIT * hid, width), jnp.bfloat16)] * 3
        + [
            pltpu.VMEM((count, SPLIT * hid), jnp.bfloat16),
            pltpu.VMEM((tile * lines, LANES), jnp.float32),
            pltpu.VMEM(everything, jnp.bfloat16),
            pltpu.SemaphoreType.DMA((3 * SPLIT,)),
            pltpu.SemaphoreType.DMA((2 * count // tile,)),
        ],
        compiler_params=pltpu.CompilerParams(vmem_limit_bytes=57 * 1024 * 1024),
        cost_estimate=pl.CostEstimate(
            flops=2 * count * width * hid * 12,
            bytes_accessed=4 * count * width + 24 * hid * width,
            transcendentals=count * hid * 4,
        ),
    )(rows, *pieces)


def pick_kernel(where_ref, *refs):
    sources, out_ref = refs[:-1], refs[-1]
    width = out_ref.shape[1]
    records = jnp.concatenate([source[...] for source in sources], axis=0)
    named = records[:, width:].astype(jnp.float32).T
    tokens = records.shape[0]
    count = tokens // len(sources)
    share = CHUNKS * MOST
    experts = out_ref.shape[0] // share
    target = pl.program_id(0) * experts + lax.broadcasted_iota(jnp.int32, (experts, tokens), 0)
    zs = SIZES[4]
    expert = (2 * (target % zs) + where_ref[0]) * 8 + 2 * (target // zs) + where_ref[1]
    expert = expert.astype(jnp.float32)
    chosen = jnp.zeros((experts, tokens), jnp.float32)
    for k in range(TOP):
        chosen = jnp.where(named[k : k + 1, :] == expert, 1.0, chosen)
    row = lax.broadcasted_iota(jnp.int32, (tokens, tokens), 0)
    column = lax.broadcasted_iota(jnp.int32, (tokens, tokens), 1)
    before = jnp.where((row // count == column // count) & (row < column), 1.0, 0.0)
    rank = jnp.dot(
        chosen.astype(jnp.bfloat16), before.astype(jnp.bfloat16), preferred_element_type=jnp.float32
    )
    chunk = lax.broadcasted_iota(jnp.int32, (experts, tokens), 1) // count
    slot = jnp.where(chosen > 0.0, rank.astype(jnp.int32) + chunk * MOST, -1)
    slots = lax.broadcasted_iota(jnp.int32, (experts, share, tokens), 1)
    hit = jnp.where(slot[:, None, :] == slots, 1.0, 0.0).reshape(experts * share, tokens)
    out_ref[...] = jnp.dot(
        hit.astype(jnp.bfloat16), records[:, :width], preferred_element_type=jnp.float32
    ).astype(jnp.bfloat16)


def pick_rows(where, sources, width):
    tokens = len(sources) * sources[0].shape[0]
    count = PLANE * CHUNKS * MOST
    steps = SIZES[0]
    whole = pl.BlockSpec(sources[0].shape, lambda i: (0, 0))
    return pl.pallas_call(
        pick_kernel,
        grid=(steps,),
        out_shape=jax.ShapeDtypeStruct((count, width), jnp.bfloat16),
        in_specs=[pl.BlockSpec(memory_space=pltpu.SMEM)] + [whole] * len(sources),
        out_specs=pl.BlockSpec((count // steps, width), lambda i: (i, 0)),
        compiler_params=pltpu.CompilerParams(vmem_limit_bytes=20 * 1024 * 1024),
        cost_estimate=pl.CostEstimate(
            flops=2 * count * tokens * width,
            bytes_accessed=2 * (count + tokens) * (width + tokens),
            transcendentals=0,
        ),
    )(where, *sources)


def sum_kernel(returned_ref, spread_ref, *refs):
    outs, (lined, rows) = refs[:-2], refs[-2:]
    count, width = rows.shape
    lines = width // LANES
    lined[...] = returned_ref[...].astype(jnp.float32)
    for n in range(lines):
        part = slice(n * LANES, (n + 1) * LANES)
        rows[:, part] = lined[pl.ds(n, count, stride=lines), :].astype(jnp.bfloat16)
    total = lax.dot_general(
        spread_ref[...], rows[...], (((0,), (0,)), ((), ())), preferred_element_type=jnp.float32
    )
    half = total.shape[0] // 2
    total = total[:half] + total[half:]
    tokens = outs[0].shape[0]
    for k, out in enumerate(outs):
        out[...] = total[k * tokens : (k + 1) * tokens].astype(jnp.bfloat16)


def sum_rows(returned, spread, planes, width):
    count = spread.shape[0]
    tokens = spread.shape[1] // 2 // planes
    return pl.pallas_call(
        sum_kernel,
        out_shape=[jax.ShapeDtypeStruct((tokens, width), jnp.bfloat16)] * planes,
        scratch_shapes=[
            pltpu.VMEM((count * width // LANES, LANES), jnp.float32),
            pltpu.VMEM((count, width), jnp.bfloat16),
        ],
        compiler_params=pltpu.CompilerParams(vmem_limit_bytes=24 * 1024 * 1024),
        cost_estimate=pl.CostEstimate(
            flops=2 * count * spread.shape[1] * width,
            bytes_accessed=2 * count * width,
            transcendentals=0,
        ),
    )(returned, spread)


def matches(named, experts):
    return named[:, :, None] == experts[None, None, :]


def ranks(chosen, count):
    order = jnp.arange(chosen.shape[0], dtype=jnp.int32)
    before = (order[:, None] // count == order[None, :] // count) & (order[None, :] < order[:, None])
    return jnp.dot(
        before.astype(jnp.bfloat16), chosen.astype(jnp.bfloat16), preferred_element_type=jnp.float32
    ).astype(jnp.int32)


def shards(tokens, routes, route_weights, gate_weight, up_weight, down_weight):
    count, width = tokens.shape
    top = routes.shape[1]
    h, p, c = (lax.axis_index(n) for n in ("h", "p", "c"))
    zs = SIZES[4]

    high = route_weights.astype(jnp.bfloat16)
    low = (route_weights - high.astype(jnp.float32)).astype(jnp.bfloat16)
    fields = (routes.astype(jnp.bfloat16), high, low)
    meta = sum(
        jnp.pad(f, ((0, 0), (top * k, EXTRA - top * (k + 1)))) for k, f in enumerate(fields)
    )
    record = jnp.concatenate([tokens, meta], axis=1)
    received = [swap(record, axes) for axes in PARTNERS]

    own = jnp.concatenate([gate_weight[0, 0], up_weight[0, 0], down_weight[0, 0]], axis=0)
    own, received[0], received[2] = lax.optimization_barrier((own, received[0], received[2]))
    axes = ("p", "b", "c")
    first = lax.ppermute(own, axes, FIRST)
    second = jnp.where(c == p, own, lax.ppermute(first, axes, SECOND))
    pieces = [first, second, swap(first, ("c",)), swap(second, ("c",))]

    records = [record] + received
    meta = jnp.concatenate([r[:, width:] for r in records], axis=0).astype(jnp.float32)
    named = meta[:, :top].astype(jnp.int32)
    weight = meta[:, top : 2 * top] + meta[:, 2 * top : 3 * top]
    target = jnp.arange(PLANE, dtype=jnp.int32)
    match = matches(named, (2 * (target % zs) + p) * 8 + 2 * (target // zs) + h)
    chosen = jnp.any(match, axis=1)
    weight = jnp.sum(jnp.where(match, weight[:, :, None], 0.0), axis=1)
    chunk = jnp.arange(CHUNKS * count, dtype=jnp.int32) // count
    slot = jnp.where(chosen, ranks(chosen, count) + (chunk * MOST)[:, None], -1).T
    slots = jnp.arange(CHUNKS * MOST, dtype=jnp.int32)
    where = jnp.stack([p, h]).astype(jnp.int32)
    sent = pick_rows(where, records, width)

    def exchange(rows):
        return lax.all_to_all(rows, ("x", "z"), 0, 0, tiled=True)

    arrived = exchange(sent.reshape(PLANE, CHUNKS * MOST, width)).reshape(-1, width)
    own_out, far_out = run_expert(arrived, pieces)

    spread = jnp.where(
        slot[:, None, :] == slots[None, :, None], weight.T[:, None, :], 0.0
    )
    upper = spread.astype(jnp.bfloat16)
    lower = (spread - upper.astype(jnp.float32)).astype(jnp.bfloat16)
    own_spread = [half[:, :MOST, :count].reshape(-1, count) for half in (upper, lower)]
    far_spread = jnp.concatenate([half[:, MOST:, count:] for half in (upper, lower)], axis=2)
    far_spread = far_spread.reshape(-1, 2 * (CHUNKS - 1) * count)
    own_spread, far_spread, own_out = lax.optimization_barrier((own_spread, far_spread, own_out))

    far_back = exchange(far_out)
    own_out, far_back = lax.optimization_barrier((own_out, far_back))
    own_back = exchange(own_out).reshape(-1, width)
    far = sum_rows(far_back.reshape(-1, LANES), far_spread, CHUNKS - 1, width)
    gained = [swap(part, names) for part, names in zip(far, PARTNERS)]
    dims = (((0,), (0,)), ((), ()))
    mixed = sum(
        lax.dot_general(half, own_back, dims, preferred_element_type=jnp.float32)
        for half in own_spread
    )
    for part in gained:
        mixed = mixed + part.astype(jnp.float32)
    return mixed.astype(jnp.bfloat16)


def solution(mesh):
    fine = Mesh(mesh.devices.reshape(SIZES), NAMES)
    rows = P(NAMES, None)
    weights = P(("x", "h", "p", "b"), ("z", "c"), None, None)
    return jax.shard_map(
        shards,
        mesh=fine,
        in_specs=(rows, rows, rows, weights, weights, weights),
        out_specs=rows,
        check_vma=False,
    )
```

```python
import jax
import jax.numpy as jnp
from jax import lax
from jax.experimental import pallas as pl
from jax.experimental.pallas import tpu as pltpu
from jax.sharding import Mesh, PartitionSpec as P

SIZES = (4, 2, 2, 2, 8, 2)
NAMES = ("x", "h", "p", "b", "z", "c")
MOST = 6
CHUNKS = 4
PLANE = 32
EXTRA = 128
LANES = 128
WIDE = 256
TOP = 8
SPLIT = 4


def flips(axes):
    return [(i, i ^ (2 ** len(axes) - 1)) for i in range(2 ** len(axes))]


def place(p, b, c):
    return p * 4 + b * 2 + c


FIRST = [
    (place(1, 0, 0), place(0, 1, 1)),
    (place(1, 1, 0), place(0, 0, 1)),
    (place(0, 1, 1), place(1, 0, 0)),
    (place(0, 0, 1), place(1, 1, 0)),
    (place(0, 0, 0), place(0, 1, 0)),
    (place(0, 1, 0), place(0, 0, 0)),
    (place(1, 0, 1), place(1, 1, 1)),
    (place(1, 1, 1), place(1, 0, 1)),
]
SECOND = [
    (place(0, 0, 1), place(0, 1, 1)),
    (place(0, 1, 1), place(0, 0, 1)),
    (place(1, 0, 0), place(1, 1, 0)),
    (place(1, 1, 0), place(1, 0, 0)),
]
PARTNERS = (("p",), ("h", "p", "b"), ("h", "b"))


def swap(value, axes):
    return lax.ppermute(value, axes, flips(axes))


def expert_kernel(rows_ref, *refs):
    pieces, (own_out, far_out) = refs[:SPLIT], refs[SPLIT : SPLIT + 2]
    panels, (hidden, lined, staged, in_sems, out_sems) = refs[6:9], refs[9:]
    hid = pieces[0].shape[0] // 3
    copies = [
        [
            pltpu.make_async_copy(
                piece.at[pl.ds(k * hid, hid)],
                panel.at[pl.ds(q * hid, hid)],
                in_sems.at[k * SPLIT + q],
            )
            for q, piece in enumerate(pieces)
        ]
        for k, panel in enumerate(panels)
    ]
    gates, ups, downs = copies
    for gate_copy, up_copy in zip(gates, ups):
        gate_copy.start()
        up_copy.start()
    for copy in downs:
        copy.start()

    gate, up, down = panels
    dims = (((1,), (1,)), ((), ()))
    rows = rows_ref[...]
    here = 0
    for start in range(0, SPLIT * hid, WIDE):
        while here * hid < start + WIDE:
            gates[here].wait()
            ups[here].wait()
            here += 1
        part = slice(start, start + WIDE)
        g = lax.dot_general(rows, gate[part, :], dims, preferred_element_type=jnp.float32)
        u = lax.dot_general(rows, up[part, :], dims, preferred_element_type=jnp.float32)
        hidden[:, part] = (g / (1.0 + jnp.exp(-g)) * u).astype(jnp.bfloat16)
    for copy in downs:
        copy.wait()

    lines = down.shape[1] // LANES
    tile = lined.shape[0] // lines
    share = CHUNKS * MOST
    sources = tile // share
    writes = []
    for k in range(rows.shape[0] // tile):
        result = jnp.dot(
            hidden[k * tile : (k + 1) * tile, :], down[...], preferred_element_type=jnp.float32
        )
        for n in range(lines):
            lined[pl.ds(n, tile, stride=lines), :] = result[:, n * LANES : (n + 1) * LANES]
        span = slice(k * sources, (k + 1) * sources)
        staged[span] = lined[...].astype(jnp.bfloat16).reshape(sources, share * lines, LANES)
        span = pl.ds(k * sources, sources)
        cut = MOST * lines
        for n, (out, part) in enumerate(
            ((own_out, pl.ds(0, cut)), (far_out, pl.ds(cut, share * lines - cut)))
        ):
            write = pltpu.make_async_copy(
                staged.at[span, part], out.at[span], out_sems.at[2 * k + n]
            )
            write.start()
            writes.append(write)
    for write in writes:
        write.wait()


def run_expert(rows, pieces):
    count, width = rows.shape
    hid = pieces[0].shape[0] // 3
    lines = width // LANES
    tile = count // 2
    cut = MOST * lines
    everything = (PLANE, CHUNKS * cut, LANES)
    return pl.pallas_call(
        expert_kernel,
        out_shape=[
            jax.ShapeDtypeStruct((PLANE, n, LANES), jnp.bfloat16) for n in (cut, (CHUNKS - 1) * cut)
        ],
        in_specs=[pl.BlockSpec(memory_space=pltpu.VMEM)]
        + [pl.BlockSpec(memory_space=pl.ANY)] * SPLIT,
        out_specs=[pl.BlockSpec(memory_space=pltpu.HBM)] * 2,
        scratch_shapes=[pltpu.VMEM((SPLIT * hid, width), jnp.bfloat16)] * 3
        + [
            pltpu.VMEM((count, SPLIT * hid), jnp.bfloat16),
            pltpu.VMEM((tile * lines, LANES), jnp.float32),
            pltpu.VMEM(everything, jnp.bfloat16),
            pltpu.SemaphoreType.DMA((3 * SPLIT,)),
            pltpu.SemaphoreType.DMA((2 * count // tile,)),
        ],
        compiler_params=pltpu.CompilerParams(vmem_limit_bytes=57 * 1024 * 1024),
        cost_estimate=pl.CostEstimate(
            flops=2 * count * width * hid * 12,
            bytes_accessed=4 * count * width + 24 * hid * width,
            transcendentals=count * hid * 4,
        ),
    )(rows, *pieces)


def pick_kernel(where_ref, *refs):
    sources, out_ref = refs[:-1], refs[-1]
    width = out_ref.shape[1]
    records = jnp.concatenate([source[...] for source in sources], axis=0)
    named = records[:, width:].astype(jnp.float32).T
    tokens = records.shape[0]
    count = tokens // len(sources)
    share = CHUNKS * MOST
    experts = out_ref.shape[0] // share
    target = pl.program_id(0) * experts + lax.broadcasted_iota(jnp.int32, (experts, tokens), 0)
    zs = SIZES[4]
    expert = (2 * (target % zs) + where_ref[0]) * 8 + 2 * (target // zs) + where_ref[1]
    expert = expert.astype(jnp.float32)
    chosen = jnp.zeros((experts, tokens), jnp.float32)
    for k in range(TOP):
        chosen = jnp.where(named[k : k + 1, :] == expert, 1.0, chosen)
    row = lax.broadcasted_iota(jnp.int32, (tokens, tokens), 0)
    column = lax.broadcasted_iota(jnp.int32, (tokens, tokens), 1)
    before = jnp.where((row // count == column // count) & (row < column), 1.0, 0.0)
    rank = jnp.dot(
        chosen.astype(jnp.bfloat16), before.astype(jnp.bfloat16), preferred_element_type=jnp.float32
    )
    chunk = lax.broadcasted_iota(jnp.int32, (experts, tokens), 1) // count
    slot = jnp.where(chosen > 0.0, rank.astype(jnp.int32) + chunk * MOST, -1)
    slots = lax.broadcasted_iota(jnp.int32, (experts, share, tokens), 1)
    hit = jnp.where(slot[:, None, :] == slots, 1.0, 0.0).reshape(experts * share, tokens)
    out_ref[...] = jnp.dot(
        hit.astype(jnp.bfloat16), records[:, :width], preferred_element_type=jnp.float32
    ).astype(jnp.bfloat16)


def pick_rows(where, sources, width):
    tokens = len(sources) * sources[0].shape[0]
    count = PLANE * CHUNKS * MOST
    steps = SIZES[0]
    whole = pl.BlockSpec(sources[0].shape, lambda i: (0, 0))
    return pl.pallas_call(
        pick_kernel,
        grid=(steps,),
        out_shape=jax.ShapeDtypeStruct((count, width), jnp.bfloat16),
        in_specs=[pl.BlockSpec(memory_space=pltpu.SMEM)] + [whole] * len(sources),
        out_specs=pl.BlockSpec((count // steps, width), lambda i: (i, 0)),
        compiler_params=pltpu.CompilerParams(vmem_limit_bytes=20 * 1024 * 1024),
        cost_estimate=pl.CostEstimate(
            flops=2 * count * tokens * width,
            bytes_accessed=2 * (count + tokens) * (width + tokens),
            transcendentals=0,
        ),
    )(where, *sources)


def sum_kernel(returned_ref, spread_ref, *refs):
    outs, (lined, rows) = refs[:-2], refs[-2:]
    count, width = rows.shape
    lines = width // LANES
    lined[...] = returned_ref[...].astype(jnp.float32)
    for n in range(lines):
        part = slice(n * LANES, (n + 1) * LANES)
        rows[:, part] = lined[pl.ds(n, count, stride=lines), :].astype(jnp.bfloat16)
    total = lax.dot_general(
        spread_ref[...], rows[...], (((0,), (0,)), ((), ())), preferred_element_type=jnp.float32
    )
    half = total.shape[0] // 2
    total = total[:half] + total[half:]
    tokens = outs[0].shape[0]
    for k, out in enumerate(outs):
        out[...] = total[k * tokens : (k + 1) * tokens].astype(jnp.bfloat16)


def sum_rows(returned, spread, planes, width):
    count = spread.shape[0]
    tokens = spread.shape[1] // 2 // planes
    return pl.pallas_call(
        sum_kernel,
        out_shape=[jax.ShapeDtypeStruct((tokens, width), jnp.bfloat16)] * planes,
        scratch_shapes=[
            pltpu.VMEM((count * width // LANES, LANES), jnp.float32),
            pltpu.VMEM((count, width), jnp.bfloat16),
        ],
        compiler_params=pltpu.CompilerParams(vmem_limit_bytes=24 * 1024 * 1024),
        cost_estimate=pl.CostEstimate(
            flops=2 * count * spread.shape[1] * width,
            bytes_accessed=2 * count * width,
            transcendentals=0,
        ),
    )(returned, spread)


def matches(named, experts):
    return named[:, :, None] == experts[None, None, :]


def ranks(chosen, count):
    order = jnp.arange(chosen.shape[0], dtype=jnp.int32)
    before = (order[:, None] // count == order[None, :] // count) & (order[None, :] < order[:, None])
    return jnp.dot(
        before.astype(jnp.bfloat16), chosen.astype(jnp.bfloat16), preferred_element_type=jnp.float32
    ).astype(jnp.int32)


def shards(tokens, routes, route_weights, gate_weight, up_weight, down_weight):
    count, width = tokens.shape
    top = routes.shape[1]
    h, p, c = (lax.axis_index(n) for n in ("h", "p", "c"))
    zs = SIZES[4]

    high = route_weights.astype(jnp.bfloat16)
    low = (route_weights - high.astype(jnp.float32)).astype(jnp.bfloat16)
    fields = (routes.astype(jnp.bfloat16), high, low)
    meta = sum(
        jnp.pad(f, ((0, 0), (top * k, EXTRA - top * (k + 1)))) for k, f in enumerate(fields)
    )
    record = jnp.concatenate([tokens, meta], axis=1)
    received = [swap(record, axes) for axes in PARTNERS]

    own = jnp.concatenate([gate_weight[0, 0], up_weight[0, 0], down_weight[0, 0]], axis=0)
    own, received = lax.optimization_barrier((own, received))
    axes = ("p", "b", "c")
    first = lax.ppermute(own, axes, FIRST)
    second = jnp.where(c == p, own, lax.ppermute(first, axes, SECOND))
    pieces = [first, second, swap(first, ("c",)), swap(second, ("c",))]

    records = [record] + received
    meta = jnp.concatenate([r[:, width:] for r in records], axis=0).astype(jnp.float32)
    named = meta[:, :top].astype(jnp.int32)
    weight = meta[:, top : 2 * top] + meta[:, 2 * top : 3 * top]
    target = jnp.arange(PLANE, dtype=jnp.int32)
    match = matches(named, (2 * (target % zs) + p) * 8 + 2 * (target // zs) + h)
    chosen = jnp.any(match, axis=1)
    weight = jnp.sum(jnp.where(match, weight[:, :, None], 0.0), axis=1)
    chunk = jnp.arange(CHUNKS * count, dtype=jnp.int32) // count
    slot = jnp.where(chosen, ranks(chosen, count) + (chunk * MOST)[:, None], -1).T
    slots = jnp.arange(CHUNKS * MOST, dtype=jnp.int32)
    where = jnp.stack([p, h]).astype(jnp.int32)
    sent = pick_rows(where, records, width)

    def exchange(rows):
        return lax.all_to_all(rows, ("x", "z"), 0, 0, tiled=True)

    arrived = exchange(sent.reshape(PLANE, CHUNKS * MOST, width)).reshape(-1, width)
    own_out, far_out = run_expert(arrived, pieces)

    spread = jnp.where(
        slot[:, None, :] == slots[None, :, None], weight.T[:, None, :], 0.0
    )
    upper = spread.astype(jnp.bfloat16)
    lower = (spread - upper.astype(jnp.float32)).astype(jnp.bfloat16)
    own_spread = [half[:, :MOST, :count].reshape(-1, count) for half in (upper, lower)]
    far_spread = jnp.concatenate([half[:, MOST:, count:] for half in (upper, lower)], axis=2)
    far_spread = far_spread.reshape(-1, 2 * (CHUNKS - 1) * count)
    own_spread, far_spread, own_out = lax.optimization_barrier((own_spread, far_spread, own_out))

    far_back = exchange(far_out)
    own_out, far_back = lax.optimization_barrier((own_out, far_back))
    own_back = exchange(own_out).reshape(-1, width)
    far = sum_rows(far_back.reshape(-1, LANES), far_spread, CHUNKS - 1, width)
    gained = [swap(part, names) for part, names in zip(far, PARTNERS)]
    dims = (((0,), (0,)), ((), ()))
    mixed = sum(
        lax.dot_general(half, own_back, dims, preferred_element_type=jnp.float32)
        for half in own_spread
    )
    for part in gained:
        mixed = mixed + part.astype(jnp.float32)
    return mixed.astype(jnp.bfloat16)


def solution(mesh):
    fine = Mesh(mesh.devices.reshape(SIZES), NAMES)
    rows = P(NAMES, None)
    weights = P(("x", "h", "p", "b"), ("z", "c"), None, None)
    return jax.shard_map(
        shards,
        mesh=fine,
        in_specs=(rows, rows, rows, weights, weights, weights),
        out_specs=rows,
        check_vma=False,
    )
```

```python
import jax
import jax.numpy as jnp
from jax import lax
from jax.experimental import pallas as pl
from jax.experimental.pallas import tpu as pltpu
from jax.sharding import Mesh, PartitionSpec as P

SIZES = (4, 2, 2, 2, 8, 2)
NAMES = ("x", "h", "p", "b", "z", "c")
MOST = 6
CHUNKS = 4
PLANE = 32
EXTRA = 128
LANES = 128
WIDE = 256
TOP = 8
SPLIT = 4


def flips(axes):
    return [(i, i ^ (2 ** len(axes) - 1)) for i in range(2 ** len(axes))]


def place(p, b, c):
    return p * 4 + b * 2 + c


FIRST = [
    (place(1, 0, 0), place(0, 1, 1)),
    (place(1, 1, 0), place(0, 0, 1)),
    (place(0, 1, 1), place(1, 0, 0)),
    (place(0, 0, 1), place(1, 1, 0)),
    (place(0, 0, 0), place(0, 1, 0)),
    (place(0, 1, 0), place(0, 0, 0)),
    (place(1, 0, 1), place(1, 1, 1)),
    (place(1, 1, 1), place(1, 0, 1)),
]
SECOND = [
    (place(0, 0, 1), place(0, 1, 1)),
    (place(0, 1, 1), place(0, 0, 1)),
    (place(1, 0, 0), place(1, 1, 0)),
    (place(1, 1, 0), place(1, 0, 0)),
]
PARTNERS = (("p",), ("h", "p", "b"), ("h", "b"))


def swap(value, axes):
    return lax.ppermute(value, axes, flips(axes))


def expert_kernel(home_ref, rows_ref, *refs):
    first, third, own, late, got, early = refs[:6]
    own_out, far_out = refs[6:8]
    panels, (hidden, lined, staged, in_sems, out_sems) = refs[8:11], refs[11:]
    hid = first.shape[0] // 3
    home = home_ref[0] == 1

    def load(piece, k, q):
        return pltpu.make_async_copy(
            piece.at[pl.ds(k * hid, hid)],
            panels[k].at[pl.ds(q * hid, hid)],
            in_sems.at[k * SPLIT + q],
        )

    def start(kinds, quarters, pieces):
        for q, piece in zip(quarters, pieces):
            for k in kinds:
                load(piece, k, q).start()

    start((0, 1), (0, 1), (first, third))

    @pl.when(home)
    def _():
        start((0, 1), (2, 3), (own, late))
        start((2,), (2, 3), (own, late))

    @pl.when(jnp.logical_not(home))
    def _():
        start((0, 1), (2, 3), (got, early))
        start((2,), (2, 3), (got, early))

    start((2,), (0, 1), (first, third))
    gates, ups, downs = [[load(first, k, q) for q in range(SPLIT)] for k in range(3)]

    gate, up, down = panels
    dims = (((1,), (1,)), ((), ()))
    rows = rows_ref[...]
    here = 0
    for start in range(0, SPLIT * hid, WIDE):
        while here * hid < start + WIDE:
            gates[here].wait()
            ups[here].wait()
            here += 1
        part = slice(start, start + WIDE)
        g = lax.dot_general(rows, gate[part, :], dims, preferred_element_type=jnp.float32)
        u = lax.dot_general(rows, up[part, :], dims, preferred_element_type=jnp.float32)
        hidden[:, part] = (g / (1.0 + jnp.exp(-g)) * u).astype(jnp.bfloat16)
    for copy in downs:
        copy.wait()

    lines = down.shape[1] // LANES
    tile = lined.shape[0] // lines
    share = CHUNKS * MOST
    sources = tile // share
    writes = []
    for k in range(rows.shape[0] // tile):
        result = jnp.dot(
            hidden[k * tile : (k + 1) * tile, :], down[...], preferred_element_type=jnp.float32
        )
        for n in range(lines):
            lined[pl.ds(n, tile, stride=lines), :] = result[:, n * LANES : (n + 1) * LANES]
        span = slice(k * sources, (k + 1) * sources)
        staged[span] = lined[...].astype(jnp.bfloat16).reshape(sources, share * lines, LANES)
        span = pl.ds(k * sources, sources)
        cut = MOST * lines
        for n, (out, part) in enumerate(
            ((own_out, pl.ds(0, cut)), (far_out, pl.ds(cut, share * lines - cut)))
        ):
            write = pltpu.make_async_copy(
                staged.at[span, part], out.at[span], out_sems.at[2 * k + n]
            )
            write.start()
            writes.append(write)
    for write in writes:
        write.wait()


def run_expert(home, rows, pieces):
    count, width = rows.shape
    hid = pieces[0].shape[0] // 3
    lines = width // LANES
    tile = count // 2
    cut = MOST * lines
    everything = (PLANE, CHUNKS * cut, LANES)
    return pl.pallas_call(
        expert_kernel,
        out_shape=[
            jax.ShapeDtypeStruct((PLANE, n, LANES), jnp.bfloat16) for n in (cut, (CHUNKS - 1) * cut)
        ],
        in_specs=[
            pl.BlockSpec(memory_space=pltpu.SMEM),
            pl.BlockSpec(memory_space=pltpu.VMEM),
        ]
        + [pl.BlockSpec(memory_space=pl.ANY)] * len(pieces),
        out_specs=[pl.BlockSpec(memory_space=pltpu.HBM)] * 2,
        scratch_shapes=[pltpu.VMEM((SPLIT * hid, width), jnp.bfloat16)] * 3
        + [
            pltpu.VMEM((count, SPLIT * hid), jnp.bfloat16),
            pltpu.VMEM((tile * lines, LANES), jnp.float32),
            pltpu.VMEM(everything, jnp.bfloat16),
            pltpu.SemaphoreType.DMA((3 * SPLIT,)),
            pltpu.SemaphoreType.DMA((2 * count // tile,)),
        ],
        compiler_params=pltpu.CompilerParams(vmem_limit_bytes=57 * 1024 * 1024),
        cost_estimate=pl.CostEstimate(
            flops=2 * count * width * hid * 12,
            bytes_accessed=4 * count * width + 24 * hid * width,
            transcendentals=count * hid * 4,
        ),
    )(home, rows, *pieces)


def pick_kernel(where_ref, *refs):
    sources, out_ref = refs[:-1], refs[-1]
    width = out_ref.shape[1]
    records = jnp.concatenate([source[...] for source in sources], axis=0)
    named = records[:, width:].astype(jnp.float32).T
    tokens = records.shape[0]
    count = tokens // len(sources)
    share = CHUNKS * MOST
    experts = out_ref.shape[0] // share
    target = pl.program_id(0) * experts + lax.broadcasted_iota(jnp.int32, (experts, tokens), 0)
    zs = SIZES[4]
    expert = (2 * (target % zs) + where_ref[0]) * 8 + 2 * (target // zs) + where_ref[1]
    expert = expert.astype(jnp.float32)
    chosen = jnp.zeros((experts, tokens), jnp.float32)
    for k in range(TOP):
        chosen = jnp.where(named[k : k + 1, :] == expert, 1.0, chosen)
    row = lax.broadcasted_iota(jnp.int32, (tokens, tokens), 0)
    column = lax.broadcasted_iota(jnp.int32, (tokens, tokens), 1)
    before = jnp.where((row // count == column // count) & (row < column), 1.0, 0.0)
    rank = jnp.dot(
        chosen.astype(jnp.bfloat16), before.astype(jnp.bfloat16), preferred_element_type=jnp.float32
    )
    chunk = lax.broadcasted_iota(jnp.int32, (experts, tokens), 1) // count
    slot = jnp.where(chosen > 0.0, rank.astype(jnp.int32) + chunk * MOST, -1)
    slots = lax.broadcasted_iota(jnp.int32, (experts, share, tokens), 1)
    hit = jnp.where(slot[:, None, :] == slots, 1.0, 0.0).reshape(experts * share, tokens)
    out_ref[...] = jnp.dot(
        hit.astype(jnp.bfloat16), records[:, :width], preferred_element_type=jnp.float32
    ).astype(jnp.bfloat16)


def pick_rows(where, sources, width):
    tokens = len(sources) * sources[0].shape[0]
    count = PLANE * CHUNKS * MOST
    steps = SIZES[0]
    whole = pl.BlockSpec(sources[0].shape, lambda i: (0, 0))
    return pl.pallas_call(
        pick_kernel,
        grid=(steps,),
        out_shape=jax.ShapeDtypeStruct((count, width), jnp.bfloat16),
        in_specs=[pl.BlockSpec(memory_space=pltpu.SMEM)] + [whole] * len(sources),
        out_specs=pl.BlockSpec((count // steps, width), lambda i: (i, 0)),
        compiler_params=pltpu.CompilerParams(vmem_limit_bytes=20 * 1024 * 1024),
        cost_estimate=pl.CostEstimate(
            flops=2 * count * tokens * width,
            bytes_accessed=2 * (count + tokens) * (width + tokens),
            transcendentals=0,
        ),
    )(where, *sources)


def sum_kernel(returned_ref, spread_ref, *refs):
    outs, (lined, rows) = refs[:-2], refs[-2:]
    count, width = rows.shape
    lines = width // LANES
    lined[...] = returned_ref[...].astype(jnp.float32)
    for n in range(lines):
        part = slice(n * LANES, (n + 1) * LANES)
        rows[:, part] = lined[pl.ds(n, count, stride=lines), :].astype(jnp.bfloat16)
    total = lax.dot_general(
        spread_ref[...], rows[...], (((0,), (0,)), ((), ())), preferred_element_type=jnp.float32
    )
    half = total.shape[0] // 2
    total = total[:half] + total[half:]
    tokens = outs[0].shape[0]
    for k, out in enumerate(outs):
        out[...] = total[k * tokens : (k + 1) * tokens].astype(jnp.bfloat16)


def sum_rows(returned, spread, planes, width):
    count = spread.shape[0]
    tokens = spread.shape[1] // 2 // planes
    return pl.pallas_call(
        sum_kernel,
        out_shape=[jax.ShapeDtypeStruct((tokens, width), jnp.bfloat16)] * planes,
        scratch_shapes=[
            pltpu.VMEM((count * width // LANES, LANES), jnp.float32),
            pltpu.VMEM((count, width), jnp.bfloat16),
        ],
        compiler_params=pltpu.CompilerParams(vmem_limit_bytes=24 * 1024 * 1024),
        cost_estimate=pl.CostEstimate(
            flops=2 * count * spread.shape[1] * width,
            bytes_accessed=2 * count * width,
            transcendentals=0,
        ),
    )(returned, spread)


def matches(named, experts):
    return named[:, :, None] == experts[None, None, :]


def ranks(chosen, count):
    order = jnp.arange(chosen.shape[0], dtype=jnp.int32)
    before = (order[:, None] // count == order[None, :] // count) & (order[None, :] < order[:, None])
    return jnp.dot(
        before.astype(jnp.bfloat16), chosen.astype(jnp.bfloat16), preferred_element_type=jnp.float32
    ).astype(jnp.int32)


def shards(tokens, routes, route_weights, gate_weight, up_weight, down_weight):
    count, width = tokens.shape
    top = routes.shape[1]
    h, p, c = (lax.axis_index(n) for n in ("h", "p", "c"))
    zs = SIZES[4]

    high = route_weights.astype(jnp.bfloat16)
    low = (route_weights - high.astype(jnp.float32)).astype(jnp.bfloat16)
    fields = (routes.astype(jnp.bfloat16), high, low)
    meta = sum(
        jnp.pad(f, ((0, 0), (top * k, EXTRA - top * (k + 1)))) for k, f in enumerate(fields)
    )
    record = jnp.concatenate([tokens, meta], axis=1)
    received = [swap(record, axes) for axes in PARTNERS]

    own = jnp.concatenate([gate_weight[0, 0], up_weight[0, 0], down_weight[0, 0]], axis=0)
    own, received = lax.optimization_barrier((own, received))
    axes = ("p", "b", "c")
    first = lax.ppermute(own, axes, FIRST)
    third = swap(first, ("c",))
    got = lax.ppermute(first, axes, SECOND)
    early = lax.ppermute(own, ("p", "c"), ((0, 1), (3, 2)))
    late = lax.ppermute(got, ("p", "c"), ((1, 0), (2, 3)))
    pieces = [first, third, own, late, got, early]
    home = (c == p).astype(jnp.int32).reshape(1)

    records = [record] + received
    meta = jnp.concatenate([r[:, width:] for r in records], axis=0).astype(jnp.float32)
    named = meta[:, :top].astype(jnp.int32)
    weight = meta[:, top : 2 * top] + meta[:, 2 * top : 3 * top]
    target = jnp.arange(PLANE, dtype=jnp.int32)
    match = matches(named, (2 * (target % zs) + p) * 8 + 2 * (target // zs) + h)
    chosen = jnp.any(match, axis=1)
    weight = jnp.sum(jnp.where(match, weight[:, :, None], 0.0), axis=1)
    chunk = jnp.arange(CHUNKS * count, dtype=jnp.int32) // count
    slot = jnp.where(chosen, ranks(chosen, count) + (chunk * MOST)[:, None], -1).T
    slots = jnp.arange(CHUNKS * MOST, dtype=jnp.int32)
    where = jnp.stack([p, h]).astype(jnp.int32)
    sent = pick_rows(where, records, width)

    def exchange(rows):
        return lax.all_to_all(rows, ("x", "z"), 0, 0, tiled=True)

    arrived = exchange(sent.reshape(PLANE, CHUNKS * MOST, width)).reshape(-1, width)
    own_out, far_out = run_expert(home, arrived, pieces)

    spread = jnp.where(
        slot[:, None, :] == slots[None, :, None], weight.T[:, None, :], 0.0
    )
    upper = spread.astype(jnp.bfloat16)
    lower = (spread - upper.astype(jnp.float32)).astype(jnp.bfloat16)
    own_spread = [half[:, :MOST, :count].reshape(-1, count) for half in (upper, lower)]
    far_spread = jnp.concatenate([half[:, MOST:, count:] for half in (upper, lower)], axis=2)
    far_spread = far_spread.reshape(-1, 2 * (CHUNKS - 1) * count)
    own_spread, far_spread, own_out = lax.optimization_barrier((own_spread, far_spread, own_out))

    far_back = exchange(far_out)
    own_out, far_back = lax.optimization_barrier((own_out, far_back))
    own_back = exchange(own_out).reshape(-1, width)
    far = sum_rows(far_back.reshape(-1, LANES), far_spread, CHUNKS - 1, width)
    gained = [swap(part, names) for part, names in zip(far, PARTNERS)]
    dims = (((0,), (0,)), ((), ()))
    mixed = sum(
        lax.dot_general(half, own_back, dims, preferred_element_type=jnp.float32)
        for half in own_spread
    )
    for part in gained:
        mixed = mixed + part.astype(jnp.float32)
    return mixed.astype(jnp.bfloat16)


def solution(mesh):
    fine = Mesh(mesh.devices.reshape(SIZES), NAMES)
    rows = P(NAMES, None)
    weights = P(("x", "h", "p", "b"), ("z", "c"), None, None)
    return jax.shard_map(
        shards,
        mesh=fine,
        in_specs=(rows, rows, rows, weights, weights, weights),
        out_specs=rows,
        check_vma=False,
    )
```

```python
import jax
import jax.numpy as jnp
from jax import lax
from jax.experimental import pallas as pl
from jax.experimental.pallas import tpu as pltpu
from jax.sharding import Mesh, PartitionSpec as P

SIZES = (4, 2, 2, 2, 8, 2)
NAMES = ("x", "h", "p", "b", "z", "c")
MOST = 6
CHUNKS = 4
PLANE = 32
EXTRA = 128
LANES = 128
WIDE = 256
TOP = 8
SPLIT = 4


def flips(axes):
    return [(i, i ^ (2 ** len(axes) - 1)) for i in range(2 ** len(axes))]


def place(p, b, c):
    return p * 4 + b * 2 + c


FIRST = [
    (place(1, 0, 0), place(0, 1, 1)),
    (place(1, 1, 0), place(0, 0, 1)),
    (place(0, 1, 1), place(1, 0, 0)),
    (place(0, 0, 1), place(1, 1, 0)),
    (place(0, 0, 0), place(0, 1, 0)),
    (place(0, 1, 0), place(0, 0, 0)),
    (place(1, 0, 1), place(1, 1, 1)),
    (place(1, 1, 1), place(1, 0, 1)),
]
SECOND = [
    (place(0, 0, 1), place(0, 1, 1)),
    (place(0, 1, 1), place(0, 0, 1)),
    (place(1, 0, 0), place(1, 1, 0)),
    (place(1, 1, 0), place(1, 0, 0)),
]
PARTNERS = (("p",), ("h", "p", "b"), ("h", "b"))


def swap(value, axes):
    return lax.ppermute(value, axes, flips(axes))


def expert_kernel(home_ref, rows_ref, *refs):
    first, third, own, late, got, early = refs[:6]
    own_out, far_out = refs[6:8]
    panels, (hidden, lined, staged, in_sems, out_sems) = refs[8:11], refs[11:]
    hid = first.shape[0] // 3
    home = home_ref[0] == 1

    def load(piece, k, q):
        return pltpu.make_async_copy(
            piece.at[pl.ds(k * hid, hid)],
            panels[k].at[pl.ds(q * hid, hid)],
            in_sems.at[k * SPLIT + q],
        )

    def start(kinds, quarters, pieces):
        for q, piece in zip(quarters, pieces):
            for k in kinds:
                load(piece, k, q).start()

    start((0, 1), (0, 1), (first, third))

    @pl.when(home)
    def _():
        start((0, 1), (2, 3), (own, late))
        start((2,), (2, 3), (own, late))

    @pl.when(jnp.logical_not(home))
    def _():
        start((0, 1), (2, 3), (got, early))
        start((2,), (2, 3), (got, early))

    start((2,), (0, 1), (first, third))
    gates, ups, downs = [[load(first, k, q) for q in range(SPLIT)] for k in range(3)]

    gate, up, down = panels
    dims = (((1,), (1,)), ((), ()))
    rows = rows_ref[...]
    here = 0
    for start in range(0, SPLIT * hid, WIDE):
        while here * hid < start + WIDE:
            gates[here].wait()
            ups[here].wait()
            here += 1
        part = slice(start, start + WIDE)
        g = lax.dot_general(rows, gate[part, :], dims, preferred_element_type=jnp.float32)
        u = lax.dot_general(rows, up[part, :], dims, preferred_element_type=jnp.float32)
        hidden[:, part] = (g / (1.0 + jnp.exp(-g)) * u).astype(jnp.bfloat16)
    for copy in downs:
        copy.wait()

    lines = down.shape[1] // LANES
    tile = lined.shape[0] // lines
    share = CHUNKS * MOST
    sources = tile // share
    writes = []
    for k in range(rows.shape[0] // tile):
        result = jnp.dot(
            hidden[k * tile : (k + 1) * tile, :], down[...], preferred_element_type=jnp.float32
        )
        for n in range(lines):
            lined[pl.ds(n, tile, stride=lines), :] = result[:, n * LANES : (n + 1) * LANES]
        span = slice(k * sources, (k + 1) * sources)
        staged[span] = lined[...].astype(jnp.bfloat16).reshape(sources, share * lines, LANES)
        span = pl.ds(k * sources, sources)
        cut = MOST * lines
        for n, (out, part) in enumerate(
            ((own_out, pl.ds(0, cut)), (far_out, pl.ds(cut, share * lines - cut)))
        ):
            write = pltpu.make_async_copy(
                staged.at[span, part], out.at[span], out_sems.at[2 * k + n]
            )
            write.start()
            writes.append(write)
    for write in writes:
        write.wait()


def run_expert(home, rows, pieces):
    count, width = rows.shape
    hid = pieces[0].shape[0] // 3
    lines = width // LANES
    tile = count // 2
    cut = MOST * lines
    everything = (PLANE, CHUNKS * cut, LANES)
    return pl.pallas_call(
        expert_kernel,
        out_shape=[
            jax.ShapeDtypeStruct((PLANE, n, LANES), jnp.bfloat16) for n in (cut, (CHUNKS - 1) * cut)
        ],
        in_specs=[
            pl.BlockSpec(memory_space=pltpu.SMEM),
            pl.BlockSpec(memory_space=pltpu.VMEM),
        ]
        + [pl.BlockSpec(memory_space=pl.ANY)] * len(pieces),
        out_specs=[pl.BlockSpec(memory_space=pltpu.HBM)] * 2,
        scratch_shapes=[pltpu.VMEM((SPLIT * hid, width), jnp.bfloat16)] * 3
        + [
            pltpu.VMEM((count, SPLIT * hid), jnp.bfloat16),
            pltpu.VMEM((tile * lines, LANES), jnp.float32),
            pltpu.VMEM(everything, jnp.bfloat16),
            pltpu.SemaphoreType.DMA((3 * SPLIT,)),
            pltpu.SemaphoreType.DMA((2 * count // tile,)),
        ],
        compiler_params=pltpu.CompilerParams(vmem_limit_bytes=57 * 1024 * 1024),
        cost_estimate=pl.CostEstimate(
            flops=2 * count * width * hid * 12,
            bytes_accessed=4 * count * width + 24 * hid * width,
            transcendentals=count * hid * 4,
        ),
    )(home, rows, *pieces)


def pick_kernel(where_ref, *refs):
    sources, metas, out_ref = refs[:CHUNKS], refs[CHUNKS:-1], refs[-1]
    records = jnp.concatenate([source[...] for source in sources], axis=0)
    named = jnp.concatenate([meta[...] for meta in metas], axis=0).astype(jnp.float32).T
    tokens = records.shape[0]
    count = tokens // len(sources)
    share = CHUNKS * MOST
    experts = out_ref.shape[0] // share
    target = pl.program_id(0) * experts + lax.broadcasted_iota(jnp.int32, (experts, tokens), 0)
    zs = SIZES[4]
    expert = (2 * (target % zs) + where_ref[0]) * 8 + 2 * (target // zs) + where_ref[1]
    expert = expert.astype(jnp.float32)
    chosen = jnp.zeros((experts, tokens), jnp.float32)
    for k in range(TOP):
        chosen = jnp.where(named[k : k + 1, :] == expert, 1.0, chosen)
    row = lax.broadcasted_iota(jnp.int32, (tokens, tokens), 0)
    column = lax.broadcasted_iota(jnp.int32, (tokens, tokens), 1)
    before = jnp.where((row // count == column // count) & (row < column), 1.0, 0.0)
    rank = jnp.dot(
        chosen.astype(jnp.bfloat16), before.astype(jnp.bfloat16), preferred_element_type=jnp.float32
    )
    chunk = lax.broadcasted_iota(jnp.int32, (experts, tokens), 1) // count
    slot = jnp.where(chosen > 0.0, rank.astype(jnp.int32) + chunk * MOST, -1)
    slots = lax.broadcasted_iota(jnp.int32, (experts, share, tokens), 1)
    hit = jnp.where(slot[:, None, :] == slots, 1.0, 0.0).reshape(experts * share, tokens)
    out_ref[...] = jnp.dot(
        hit.astype(jnp.bfloat16), records, preferred_element_type=jnp.float32
    ).astype(jnp.bfloat16)


def pick_rows(where, sources, metas, width):
    tokens = len(sources) * sources[0].shape[0]
    count = PLANE * CHUNKS * MOST
    steps = SIZES[0]
    whole = [pl.BlockSpec(source.shape, lambda i: (0, 0)) for source in sources + metas]
    return pl.pallas_call(
        pick_kernel,
        grid=(steps,),
        out_shape=jax.ShapeDtypeStruct((count, width), jnp.bfloat16),
        in_specs=[pl.BlockSpec(memory_space=pltpu.SMEM)] + whole,
        out_specs=pl.BlockSpec((count // steps, width), lambda i: (i, 0)),
        compiler_params=pltpu.CompilerParams(vmem_limit_bytes=20 * 1024 * 1024),
        cost_estimate=pl.CostEstimate(
            flops=2 * count * tokens * width,
            bytes_accessed=2 * (count + tokens) * (width + tokens),
            transcendentals=0,
        ),
    )(where, *sources, *metas)


def sum_kernel(returned_ref, spread_ref, *refs):
    outs, (lined, rows) = refs[:-2], refs[-2:]
    count, width = rows.shape
    lines = width // LANES
    lined[...] = returned_ref[...].astype(jnp.float32)
    for n in range(lines):
        part = slice(n * LANES, (n + 1) * LANES)
        rows[:, part] = lined[pl.ds(n, count, stride=lines), :].astype(jnp.bfloat16)
    total = lax.dot_general(
        spread_ref[...], rows[...], (((0,), (0,)), ((), ())), preferred_element_type=jnp.float32
    )
    half = total.shape[0] // 2
    total = total[:half] + total[half:]
    tokens = outs[0].shape[0]
    for k, out in enumerate(outs):
        out[...] = total[k * tokens : (k + 1) * tokens].astype(jnp.bfloat16)


def sum_rows(returned, spread, planes, width):
    count = spread.shape[0]
    tokens = spread.shape[1] // 2 // planes
    return pl.pallas_call(
        sum_kernel,
        out_shape=[jax.ShapeDtypeStruct((tokens, width), jnp.bfloat16)] * planes,
        scratch_shapes=[
            pltpu.VMEM((count * width // LANES, LANES), jnp.float32),
            pltpu.VMEM((count, width), jnp.bfloat16),
        ],
        compiler_params=pltpu.CompilerParams(vmem_limit_bytes=24 * 1024 * 1024),
        cost_estimate=pl.CostEstimate(
            flops=2 * count * spread.shape[1] * width,
            bytes_accessed=2 * count * width,
            transcendentals=0,
        ),
    )(returned, spread)


def matches(named, experts):
    return named[:, :, None] == experts[None, None, :]


def ranks(chosen, count):
    order = jnp.arange(chosen.shape[0], dtype=jnp.int32)
    before = (order[:, None] // count == order[None, :] // count) & (order[None, :] < order[:, None])
    return jnp.dot(
        before.astype(jnp.bfloat16), chosen.astype(jnp.bfloat16), preferred_element_type=jnp.float32
    ).astype(jnp.int32)


def shards(tokens, routes, route_weights, gate_weight, up_weight, down_weight):
    count, width = tokens.shape
    top = routes.shape[1]
    h, p, c = (lax.axis_index(n) for n in ("h", "p", "c"))
    zs = SIZES[4]

    high = route_weights.astype(jnp.bfloat16)
    low = (route_weights - high.astype(jnp.float32)).astype(jnp.bfloat16)
    fields = (routes.astype(jnp.bfloat16), high, low)
    meta = sum(
        jnp.pad(f, ((0, 0), (top * k, EXTRA - top * (k + 1)))) for k, f in enumerate(fields)
    )
    received = [swap(tokens, axes) for axes in PARTNERS]
    meta, received[0] = lax.optimization_barrier((meta, received[0]))
    metas = [meta] + [swap(meta, axes) for axes in PARTNERS]

    own = jnp.concatenate([gate_weight[0, 0], up_weight[0, 0], down_weight[0, 0]], axis=0)
    own, received, metas = lax.optimization_barrier((own, received, metas))
    axes = ("p", "b", "c")
    first = lax.ppermute(own, axes, FIRST)
    third = swap(first, ("c",))
    got = lax.ppermute(first, axes, SECOND)
    early = lax.ppermute(own, ("p", "c"), ((0, 1), (3, 2)))
    late = lax.ppermute(got, ("p", "c"), ((1, 0), (2, 3)))
    pieces = [first, third, own, late, got, early]
    home = (c == p).astype(jnp.int32).reshape(1)

    meta = jnp.concatenate(metas, axis=0).astype(jnp.float32)
    named = meta[:, :top].astype(jnp.int32)
    weight = meta[:, top : 2 * top] + meta[:, 2 * top : 3 * top]
    target = jnp.arange(PLANE, dtype=jnp.int32)
    match = matches(named, (2 * (target % zs) + p) * 8 + 2 * (target // zs) + h)
    chosen = jnp.any(match, axis=1)
    weight = jnp.sum(jnp.where(match, weight[:, :, None], 0.0), axis=1)
    chunk = jnp.arange(CHUNKS * count, dtype=jnp.int32) // count
    slot = jnp.where(chosen, ranks(chosen, count) + (chunk * MOST)[:, None], -1).T
    slots = jnp.arange(CHUNKS * MOST, dtype=jnp.int32)
    where = jnp.stack([p, h]).astype(jnp.int32)
    sent = pick_rows(where, [tokens] + received, metas, width)

    def exchange(rows):
        return lax.all_to_all(rows, ("x", "z"), 0, 0, tiled=True)

    arrived = exchange(sent.reshape(PLANE, CHUNKS * MOST, width)).reshape(-1, width)
    own_out, far_out = run_expert(home, arrived, pieces)

    spread = jnp.where(
        slot[:, None, :] == slots[None, :, None], weight.T[:, None, :], 0.0
    )
    upper = spread.astype(jnp.bfloat16)
    lower = (spread - upper.astype(jnp.float32)).astype(jnp.bfloat16)
    own_spread = [half[:, :MOST, :count].reshape(-1, count) for half in (upper, lower)]
    far_spread = jnp.concatenate([half[:, MOST:, count:] for half in (upper, lower)], axis=2)
    far_spread = far_spread.reshape(-1, 2 * (CHUNKS - 1) * count)
    own_spread, far_spread, own_out = lax.optimization_barrier((own_spread, far_spread, own_out))

    far_back = exchange(far_out)
    own_out, far_back = lax.optimization_barrier((own_out, far_back))
    own_back = exchange(own_out).reshape(-1, width)
    far = sum_rows(far_back.reshape(-1, LANES), far_spread, CHUNKS - 1, width)
    gained = [swap(part, names) for part, names in zip(far, PARTNERS)]
    dims = (((0,), (0,)), ((), ()))
    mixed = sum(
        lax.dot_general(half, own_back, dims, preferred_element_type=jnp.float32)
        for half in own_spread
    )
    for part in gained:
        mixed = mixed + part.astype(jnp.float32)
    return mixed.astype(jnp.bfloat16)


def solution(mesh):
    fine = Mesh(mesh.devices.reshape(SIZES), NAMES)
    rows = P(NAMES, None)
    weights = P(("x", "h", "p", "b"), ("z", "c"), None, None)
    return jax.shard_map(
        shards,
        mesh=fine,
        in_specs=(rows, rows, rows, weights, weights, weights),
        out_specs=rows,
        check_vma=False,
    )
```
